512 devices in a mesh: row: 32 (over y, x), col: 16 (over z, core).
Axes of the slice: x: 4, y: 8, z: 8, core: 2. Of those that a mesh axis runs over, the one named last changes fastest.
Arguments:
- noise: bfloat16 [4096, 16384], P('row', 'col'), as said below
- data: bfloat16 [4096, 16384], P('col', 'row'), may hold values from -5 to 5
Outputs:
- targets: bfloat16 [4096, 16384], P(('row', 'col'))
- noise_potential: float32 [4096], P('row')
- data_potential: float32 [4096], P('col')
The draws below stay inside these ranges and needn't reach their ends.
Inputs may be any that keep to these rules, and one draw needn't show every extreme that they name: noise latents, real values of order one.
All inputs are finite; a program needn't handle non-finite values.
Results may differ from the reference program's by a relative error of at most 0.022.
Values may be sent and summed in bfloat16 or wider, within the bound.
A program may use at most 64 MiB of HBM per device.

```python
import math
import jax
import jax.numpy as jnp
from jax import lax

LATENT = 16384
ITERS = 3
DATA_DEV = 256
NOISE = 4096
DATA = 4096
N_COL = 16


def data_latents(key):
    return jnp.clip(jax.random.normal(key, (DATA, LATENT), jnp.float32), -5.0, 5.0)


def draw_data(key, part):
    shared = data_latents(key)
    return shared.astype(jnp.bfloat16)


def draw_noise(key, part):
    key = jax.random.fold_in(key, 7)
    first = jax.random.fold_in(key, 0)
    values = jnp.clip(jax.random.normal(first, (NOISE, LATENT), jnp.float32), -5.0, 5.0)
    return values.astype(jnp.bfloat16)


def setup_inputs(seed: int = 0) -> dict:
    splits = jax.random.split(jax.random.key(seed), 3)
    noise = draw_noise(jax.random.fold_in(splits[2], 71), 0)
    data = draw_data(jax.random.fold_in(splits[2], 71), 0)
    return dict(noise=noise, data=data)


def soft_max_log(scores, axis):
    peak = lax.optimization_barrier(jnp.max(scores, axis=axis, keepdims=True))
    return jnp.squeeze(peak, axis) + jnp.log(lax.optimization_barrier(jnp.sum(jnp.exp(scores - peak), axis=axis)))

def reference(noise, data):
    epsilon = 0.64 / math.sqrt(LATENT)
    noise_norm = lax.optimization_barrier(jnp.sum(jnp.square(noise.astype(jnp.float32)), axis=1)) / LATENT
    data_norm = lax.optimization_barrier(jnp.sum(jnp.square(data.astype(jnp.float32)), axis=1)) / LATENT
    cross = lax.dot_general(noise, data, (((1,), (1,)), ((), ())), preferred_element_type=jnp.float32)
    cost_tile = noise_norm[:, None] + data_norm[None, :] - 2.0 / LATENT * cross
    log_noise = math.log(NOISE)
    log_data = math.log(DATA)

    def row_update(data_pot):
        return -epsilon * (log_noise + soft_max_log((data_pot[None, :] - cost_tile) / epsilon, 1))

    def col_update(noise_pot):
        return -epsilon * (log_data + soft_max_log((noise_pot[:, None] - cost_tile) / epsilon, 0))
    data_pot = jnp.zeros((DATA,), jnp.float32)
    for step in range(ITERS):
        noise_pot = row_update(data_pot)
        data_pot = col_update(noise_pot)
    noise_pot = row_update(data_pot)
    weights = jnp.exp((noise_pot[:, None] + data_pot[None, :] - cost_tile) / epsilon + log_noise).astype(jnp.bfloat16)

    def add_block(index, summed):
        begin = (index * DATA_DEV).astype(jnp.int32)
        block_weights = lax.dynamic_slice_in_dim(weights, begin, DATA_DEV, 1)
        block_data = lax.dynamic_slice_in_dim(data, begin, DATA_DEV, 0)
        partial_sum = jnp.dot(block_weights, block_data, preferred_element_type=jnp.float32).astype(jnp.bfloat16)
        partial_sum = lax.optimization_barrier(partial_sum)
        return summed + partial_sum.astype(jnp.float32)
    summed = lax.fori_loop(0, N_COL, add_block, jnp.zeros((NOISE, LATENT), jnp.float32))
    return (summed.astype(jnp.bfloat16), noise_pot, data_pot)
```

```python
import functools
import math

import jax
import jax.numpy as jnp
from jax import lax
from jax.experimental import pallas as pl
from jax.experimental.pallas import tpu as pltpu
from jax.sharding import PartitionSpec as P

LATENT = 16384
ITERS = 3
MESH = pl.DeviceIdType.MESH


def flip(line, copies):
    return jnp.transpose(jnp.broadcast_to(line, (copies, line.shape[1])))


def merge(slots_ref, step, log_count):
    peaks = slots_ref[step, :, 0, :]
    sums = slots_ref[step, :, 1, :]
    peak = jnp.max(peaks, axis=0, keepdims=True)
    total = jnp.sum(sums * jnp.exp(peaks - peak), axis=0, keepdims=True)
    return -(log_count + peak + jnp.log(total))


def sinkhorn_kernel(
    n_row, n_col, log_noise, log_data, cross_ref, data_norm_ref,
    weights_ref, u_ref, v_ref,
    score, score_t, f_slots, g_slots, f_send, f_recv, g_send, g_recv,
):
    row, col = lax.axis_index("row"), lax.axis_index("col")
    epsilon = 0.64 / math.sqrt(LATENT)

    def along_col(k):
        return (row, lax.rem(col + k, n_col))

    def along_row(k):
        return (lax.rem(row + k, n_row), col)

    barrier = pltpu.get_barrier_semaphore()

    @pl.loop(1, n_col)
    def _(k):
        pl.semaphore_signal(barrier, inc=1, device_id=along_col(k), device_id_type=MESH)

    @pl.loop(1, n_row)
    def _(k):
        pl.semaphore_signal(barrier, inc=1, device_id=along_row(k), device_id_type=MESH)

    score[...] = cross_ref[...] * (2.0 / LATENT / epsilon)
    score_t[...] = jnp.transpose(score[...])
    pl.semaphore_wait(barrier, n_col + n_row - 2)

    def exchange(scores, slots, step, count, target, send, recv):
        peak = jnp.max(scores, axis=0, keepdims=True)
        slots[step, 0, 0:1, :] = peak
        slots[step, 0, 1:2, :] = jnp.sum(jnp.exp(scores - peak), axis=0, keepdims=True)

        @pl.loop(1, count)
        def _(k):
            pltpu.make_async_remote_copy(
                src_ref=slots.at[step, 0], dst_ref=slots.at[step, k],
                send_sem=send.at[step], recv_sem=recv.at[step],
                device_id=target(k), device_id_type=MESH,
            ).start()

        others = slots.at[step, pl.ds(1, count - 1)]
        pltpu.make_async_copy(others, others, recv.at[step]).wait()

    def drain(slots, step, count, send):
        others = slots.at[step, pl.ds(1, count - 1)]
        pltpu.make_async_copy(others, others, send.at[step]).wait()

    def noise_update(step, v):
        scores = score_t[...] + flip(v, score_t.shape[1])
        exchange(scores, f_slots, step, n_col, along_col, f_send, f_recv)
        return merge(f_slots, step, log_data)

    def data_update(step, u):
        rows = flip(u, 128)
        scores = score[...] + jnp.concatenate([rows] * (score.shape[1] // 128), axis=1)
        exchange(scores, g_slots, step, n_row, along_row, g_send, g_recv)
        return merge(g_slots, step, log_noise)

    v = -data_norm_ref[...] / epsilon
    for step in range(ITERS):
        u = noise_update(step, v)
        v = data_update(step, u)
    u = noise_update(ITERS, v)
    u_ref[...] = u
    v_ref[...] = v
    rows = flip(u, 128)
    rows = jnp.concatenate([rows] * (score.shape[1] // 128), axis=1)
    weights_ref[...] = jnp.exp(score[...] + rows + v + log_noise).astype(jnp.bfloat16)
    for step in range(ITERS + 1):
        drain(f_slots, step, n_col, f_send)
    for step in range(ITERS):
        drain(g_slots, step, n_row, g_send)


def per_device(noise, data):
    n_row, n_col = lax.axis_size("row"), lax.axis_size("col")
    epsilon = 0.64 / math.sqrt(LATENT)
    contract = (((1,), (1,)), ((), ()))
    noise_full = lax.all_gather(noise, "col", axis=1, tiled=True)
    noise_norm = jnp.sum(jnp.square(noise_full.astype(jnp.float32)), axis=1) / LATENT
    rows, cols = noise.shape[0], data.shape[0]
    data_full = lax.all_gather(data, "row", axis=1, tiled=True)
    data_norm = jnp.sum(jnp.square(data_full.astype(jnp.float32)), axis=1) / LATENT
    cross = lax.dot_general(noise_full, data_full, contract, preferred_element_type=jnp.float32)
    vmem = pl.BlockSpec(memory_space=pltpu.VMEM)
    dma = pltpu.SemaphoreType.DMA
    weights, u, v = pl.pallas_call(
        functools.partial(
            sinkhorn_kernel, n_row, n_col, math.log(rows * n_row), math.log(cols * n_col)
        ),
        out_shape=(
            jax.ShapeDtypeStruct((rows, cols), jnp.bfloat16),
            jax.ShapeDtypeStruct((1, rows), jnp.float32),
            jax.ShapeDtypeStruct((1, cols), jnp.float32),
        ),
        in_specs=[vmem, vmem],
        out_specs=(vmem, vmem, vmem),
        scratch_shapes=[
            pltpu.VMEM((rows, cols), jnp.float32),
            pltpu.VMEM((cols, rows), jnp.float32),
            pltpu.VMEM((ITERS + 1, n_col, 2, rows), jnp.float32),
            pltpu.VMEM((ITERS, n_row, 2, cols), jnp.float32),
            dma((ITERS + 1,)), dma((ITERS + 1,)), dma((ITERS,)), dma((ITERS,)),
        ],
        compiler_params=pltpu.CompilerParams(
            collective_id=0, has_side_effects=True, vmem_limit_bytes=16 * 2**20
        ),
        name="sinkhorn",
    )(cross, data_norm[None, :])
    noise_pot = epsilon * u[0] + noise_norm
    data_pot = epsilon * v[0] + data_norm
    targets = lax.psum_scatter(
        jnp.dot(weights, data_full, preferred_element_type=jnp.float32).astype(jnp.bfloat16),
        "col",
        scatter_dimension=0,
        tiled=True,
    )
    return (targets, noise_pot, data_pot)


def solution(mesh):
    placed = (P("row", "col"), P("col", "row"))
    return jax.shard_map(
        per_device,
        mesh=mesh,
        in_specs=placed,
        out_specs=(P(("row", "col"), None), P("row"), P("col")),
        check_vma=False,
    )
```

```python
import math

import jax
import jax.numpy as jnp
from jax import lax
from jax.experimental import pallas as pl
from jax.experimental.pallas import tpu as pltpu
from jax.sharding import PartitionSpec as P

LATENT = 16384
ITERS = 3
X, Y, Z = 4, 8, 8
N_ROW, N_COL = X * Y, 2 * Z
ROWS, COLS = 128, 256
LOG_COUNT = math.log(4096)
EPSILON = 0.64 / math.sqrt(LATENT)
BLOCK = 512
MESH = pl.DeviceIdType.MESH
F32, BF16 = jnp.float32, jnp.bfloat16


def flip(line, copies):
    return jnp.transpose(jnp.broadcast_to(line, (copies, line.shape[1])))


def squares(block):
    block = jnp.square(block.astype(F32))
    return sum(block[:, i : i + 128] for i in range(0, block.shape[1], 128))


def hops(way, half):
    return 4 if way == half else 3


def kernel(
    noise_ref, data_ref, out_ref, noise_pot_ref, data_pot_ref,
    nb, dd, part, part_in, square_sum, norm_slots, score, score_t, f_slots, g_slots,
    w_send, w_all, po, rs_in, rs_out, fin_send, fin_in,
    own_send, own_recv, ring_send, ring_recv, pair_send, pair_recv, dpair_send, dpair_recv,
    part_s, part_r, norm_s, norm_r, f_send, f_recv, g_send, g_recv, w_s, w_r,
    rs_s, rs_r, fin_s, fin_r,
):
    row, col = lax.axis_index("row"), lax.axis_index("col")
    y, x = row // X, lax.rem(row, X)
    z, c = col // 2, lax.rem(col, 2)
    other = 1 - c

    def at(y_, x_, z_, c_):
        return (y_ * X + x_, z_ * 2 + c_)

    def wrap(i, n):
        return lax.rem(i + n, n)

    def send(src, dst, send_sem, recv_sem, device):
        return pltpu.make_async_remote_copy(
            src_ref=src, dst_ref=dst, send_sem=send_sem, recv_sem=recv_sem,
            device_id=device, device_id_type=MESH,
        )

    def take(ref, sem):
        pltpu.make_async_copy(ref, ref, sem).wait()

    barrier = pltpu.get_barrier_semaphore()
    near = [at(wrap(y + 1, Y), x, z, c), at(wrap(y - 1, Y), x, z, c)]
    near += [at(y, x, wrap(z + 1, Z), c), at(y, x, wrap(z - 1, Z), c), at(y, x, z, other)]
    for k in range(1, X):
        near += [at(y, wrap(x + k, X), z, c), at(y, wrap(x + k, X), z, other)]
    for device in near:
        pl.semaphore_signal(barrier, inc=1, device_id=device, device_id_type=MESH)
    dd[c, y] = data_ref[...]
    pl.semaphore_wait(barrier, len(near))

    def ring(kind, way, half, step):
        place = (y, z)[kind]
        sign = 1 - 2 * way
        block = wrap(place - sign * (step - 1), 8)
        target = wrap(place + sign, 8)
        if kind == 0:
            ref = dd.at[c, block, pl.ds(half * 128, 128)]
            device = at(target, x, z, c)
        else:
            ref = nb.at[block, pl.ds(pl.multiple_of(c * 256 + half * 128, 128), 128)]
            device = at(y, x, target, c)
        index = (kind, way, half, step - 1)
        return send(ref, ref, ring_send.at[index], ring_recv.at[index], device)

    for half in range(2):
        for way in range(2):
            ring(0, way, half, 1).start()

    mine = x // 2 == c
    n1_device = [at(y, 2 * c + h, z, x // 2) for h in range(2)]
    n1_self = [jnp.logical_and(mine, lax.rem(x, 2) == h) for h in range(2)]
    n1_dst = nb.at[z, pl.ds(pl.multiple_of(x * ROWS, ROWS), ROWS)]
    n1_sem = own_recv.at[lax.rem(x, 2)]
    n1 = []
    for h in range(2):
        src = noise_ref.at[:, pl.ds(h * BLOCK, BLOCK)]
        far = send(src, n1_dst, own_send.at[h], n1_sem, n1_device[h])
        near_copy = pltpu.make_async_copy(src, n1_dst, n1_sem)
        n1.append(far)

        @pl.when(n1_self[h])
        def _():
            near_copy.start()

        @pl.when(jnp.logical_not(n1_self[h]))
        def _():
            far.start()

    def half_of(block, core, half):
        return nb.at[block, pl.ds(pl.multiple_of(core * 256 + half * 128, 128), 128)]

    def pair(way, half, step, block):
        index = (way, half, step)
        ref = half_of(block, c, half)
        return send(ref, ref, pair_send.at[index], pair_recv.at[index], at(y, x, z, other))

    pairs = []
    for half in range(2):
        take(half_of(z, c, half), own_recv.at[half])
        for way in range(2):
            ring(1, way, half, 1).start()
        pairs.append(pair(0, half, 0, z))
        pairs[-1].start()

    square_sum[...] = squares(data_ref[...])
    for step in range(1, 5):
        for kind in range(2):
            for half in range(2):
                for way in range(2):
                    if step > hops(way, half):
                        continue
                    arrived = ring(kind, way, half, step)
                    arrived.wait_recv()
                    if step < hops(way, half):
                        ring(kind, way, half, step + 1).start()
                    if kind == 1:
                        block = wrap(z - (1 - 2 * way) * step, Z)
                        pairs.append(pair(way, half, step, block))
                        pairs[-1].start()
        if step < 4:
            for block in (wrap(y - step, Y), wrap(y + step, Y)):
                square_sum[...] += squares(dd[c, block])
    for copy in pairs:
        copy.wait_recv()

    part[...] = jnp.zeros_like(part)

    @pl.loop(0, Y)
    def _(k):
        part[...] += lax.dot_general(
            nb[k], dd[c, k], (((1,), (1,)), ((), ())), preferred_element_type=F32
        )

    part_copies = []
    for k in (2, 1, 3):
        target = wrap(x + k, X)
        copy = send(
            part.at[pl.ds(pl.multiple_of(target * ROWS, ROWS), ROWS)], part_in.at[k - 1],
            part_s.at[k - 1], part_r.at[k - 1], at(y, target, z, c),
        )
        copy.start()
        part_copies.append(copy)
    square_sum[...] += squares(dd[c, wrap(y + 4, Y)])
    norm_slots[x] = jnp.sum(jnp.transpose(square_sum[...]), axis=0, keepdims=True)
    for k in range(1, X):
        send(
            norm_slots.at[x], norm_slots.at[x], norm_s, norm_r, at(y, wrap(x + k, X), z, c)
        ).start()
    fold = squares(noise_ref[...])
    noise_squares = jnp.sum(jnp.transpose(fold), axis=0, keepdims=True)
    for copy in part_copies:
        copy.wait_recv()
    total = part[pl.ds(pl.multiple_of(x * ROWS, ROWS), ROWS), :]
    total = total + part_in[0] + part_in[1] + part_in[2]
    score[...] = total * (2.0 / LATENT / EPSILON)
    score_t[...] = jnp.transpose(score[...])
    take(norm_slots.at[pl.ds(0, X - 1)], norm_r)
    data_norm = (norm_slots[0] + norm_slots[1] + norm_slots[2] + norm_slots[3]) / LATENT

    dpair = send(dd.at[c], dd.at[c], dpair_send, dpair_recv, at(y, x, z, other))
    dpair.start()

    def along_col(k):
        return (row, lax.rem(col + k, N_COL))

    def along_row(k):
        return (lax.rem(row + k, N_ROW), col)

    def exchange(scores, slots, step, me, count, target, send_sem, recv_sem):
        peak = jnp.max(scores, axis=0, keepdims=True)
        slots[step, me, 0:1, :] = peak
        slots[step, me, 1:2, :] = jnp.sum(jnp.exp(scores - peak), axis=0, keepdims=True)

        @pl.loop(1, count)
        def _(k):
            ref = slots.at[step, me]
            send(ref, ref, send_sem.at[step], recv_sem.at[step], target(k)).start()

        take(slots.at[step, pl.ds(0, count - 1)], recv_sem.at[step])
        peaks, sums = slots[step, :, 0, :], slots[step, :, 1, :]
        peak = jnp.max(peaks, axis=0, keepdims=True)
        total = jnp.sum(sums * jnp.exp(peaks - peak), axis=0, keepdims=True)
        return -(LOG_COUNT + peak + jnp.log(total))

    def wide(u):
        tile = flip(u, 128)
        return jnp.concatenate([tile] * (COLS // 128), axis=1)

    def noise_update(step, v):
        f_slots[step, col, 2:3, :] = noise_squares
        scores = score_t[...] + flip(v, ROWS)
        return exchange(scores, f_slots, step, col, N_COL, along_col, f_send, f_recv)

    def data_update(step, u):
        scores = score[...] + wide(u)
        return exchange(scores, g_slots, step, row, N_ROW, along_row, g_send, g_recv)

    v = -data_norm / EPSILON
    for step in range(ITERS):
        u = noise_update(step, v)
        v = data_update(step, u)
    u = noise_update(ITERS, v)

    weights = jnp.exp(score[...] + wide(u) + v + LOG_COUNT).reshape(Z, 2, 8, COLS)
    for core in range(2):
        w_send[core] = weights[:, core].reshape(Z * 8, COLS).astype(BF16)
    for k in range(X):
        for flipped in range(2):
            if k == 0 and flipped == 0:
                continue
            core = wrap(c + flipped, 2)
            send(
                w_send.at[core], w_all.at[c * X + x], w_s, w_r, at(y, wrap(x + k, X), z, core)
            ).start()
    w_all[c * X + x] = w_send[c]
    noise_norm = jnp.sum(f_slots[0, :, 2, :], axis=0, keepdims=True) / LATENT
    noise_pot_ref[...] = EPSILON * u + noise_norm
    data_pot_ref[...] = EPSILON * v + data_norm
    dpair.wait_recv()
    take(w_all.at[pl.ds(0, 2 * X - 1)], w_r)

    def rs(way, half, step):
        sign = 1 - 2 * way
        index = (way, half, step - 1)
        if step == 1:
            src = po.at[half, wrap(z + sign * hops(way, half), Z)]
        else:
            src = rs_out.at[way, half, step - 2]
        return send(
            src, rs_in.at[index], rs_s.at[index], rs_r.at[index], at(y, x, wrap(z + sign, Z), c)
        )

    for half in range(2):
        @pl.loop(0, Y // 2)
        def _(j):
            block = half * (Y // 2) + j
            sums = jnp.dot(
                w_all[0:X].reshape(256, COLS), dd[0, block], preferred_element_type=F32
            ) + jnp.dot(w_all[X:].reshape(256, COLS), dd[1, block], preferred_element_type=F32)
            sums = sums.reshape(X, Z, 8, BLOCK)
            columns = pl.ds(pl.multiple_of(j * BLOCK, BLOCK), BLOCK)
            for k in range(Z):
                po[half, k, :, columns] = sums[:, k].reshape(X * 8, BLOCK).astype(BF16)

        for way in range(2):
            rs(way, half, 1).start()

    for step in range(1, 5):
        for half in range(2):
            for way in range(2):
                if step > hops(way, half):
                    continue
                rs(way, half, step).wait_recv()
                if step < hops(way, half):
                    target = wrap(z + (1 - 2 * way) * (hops(way, half) - step), Z)
                    rs_out[way, half, step - 1] = (
                        rs_in[way, half, step - 1].astype(F32) + po[half, target].astype(F32)
                    ).astype(BF16)
                    rs(way, half, step + 1).start()
    for half in range(2):
        sums = po[half, z].astype(F32)
        for way in range(2):
            sums = sums + rs_in[way, half, hops(way, half) - 1].astype(F32)
        for k in range(X):
            lines = sums[k * 8 : k * 8 + 8]
            lines = jnp.concatenate([lines[:, :1024], lines[:, 1024:]], axis=0)
            fin_send[half, k] = lines.astype(BF16)
        fin_in[half, x] = fin_send[half, x]
        for k in range(1, X):
            target = wrap(x + k, X)
            send(
                fin_send.at[half, target], fin_in.at[half, x], fin_s.at[half], fin_r.at[half],
                at(y, target, z, c),
            ).start()
    for half in range(2):
        take(fin_in.at[half, pl.ds(0, X - 1)], fin_r.at[half])
        for k in range(X):
            lines = fin_in[half, k].astype(F32)
            for quarter in range(2):
                for part_block in range(2):
                    block = half * 4 + quarter * 2 + part_block
                    begin = (block * X + k) * BLOCK
                    out_ref[:, begin : begin + BLOCK] = lines[
                        quarter * 8 : quarter * 8 + 8, part_block * BLOCK : (part_block + 1) * BLOCK
                    ].astype(BF16)

    for h in range(2):
        @pl.when(jnp.logical_not(n1_self[h]))
        def _():
            n1[h].wait_send()
    for kind in range(2):
        for half in range(2):
            for way in range(2):
                for step in range(1, hops(way, half) + 1):
                    ring(kind, way, half, step).wait_send()
                    if kind == 0:
                        rs(way, half, step).wait_send()
    for copy in pairs + part_copies + [dpair]:
        copy.wait_send()
    take(norm_slots.at[pl.ds(0, X - 1)], norm_s)
    take(w_all.at[pl.ds(0, 2 * X - 1)], w_s)
    for half in range(2):
        take(fin_in.at[half, pl.ds(0, X - 1)], fin_s.at[half])
    for step in range(ITERS + 1):
        take(f_slots.at[step, pl.ds(0, N_COL - 1)], f_send.at[step])
    for step in range(ITERS):
        take(g_slots.at[step, pl.ds(0, N_ROW - 1)], g_send.at[step])


def per_device(noise, data):
    vmem = pl.BlockSpec(memory_space=pltpu.VMEM)
    dma = pltpu.SemaphoreType.DMA
    targets, noise_pot, data_pot = pl.pallas_call(
        kernel,
        out_shape=(
            jax.ShapeDtypeStruct((8, LATENT), BF16),
            jax.ShapeDtypeStruct((1, ROWS), F32),
            jax.ShapeDtypeStruct((1, COLS), F32),
        ),
        in_specs=[vmem, vmem],
        out_specs=(vmem, vmem, vmem),
        scratch_shapes=[
            pltpu.VMEM((Z, X * ROWS, BLOCK), BF16),
            pltpu.VMEM((2, Y, COLS, BLOCK), BF16),
            pltpu.VMEM((X * ROWS, COLS), F32),
            pltpu.VMEM((X - 1, ROWS, COLS), F32),
            pltpu.VMEM((COLS, 128), F32),
            pltpu.VMEM((X, 1, COLS), F32),
            pltpu.VMEM((ROWS, COLS), F32),
            pltpu.VMEM((COLS, ROWS), F32),
            pltpu.VMEM((ITERS + 1, N_COL, 3, ROWS), F32),
            pltpu.VMEM((ITERS, N_ROW, 2, COLS), F32),
            pltpu.VMEM((2, Z * 8, COLS), BF16),
            pltpu.VMEM((2 * X, Z * 8, COLS), BF16),
            pltpu.VMEM((2, Z, X * 8, 2048), BF16),
            pltpu.VMEM((2, 2, 4, X * 8, 2048), BF16),
            pltpu.VMEM((2, 2, 3, X * 8, 2048), BF16),
            pltpu.VMEM((2, X, 16, 1024), BF16),
            pltpu.VMEM((2, X, 16, 1024), BF16),
            dma((2,)), dma((2,)), dma((2, 2, 2, 4)), dma((2, 2, 2, 4)),
            dma((2, 2, 5)), dma((2, 2, 5)), dma, dma,
            dma((3,)), dma((3,)), dma, dma,
            dma((ITERS + 1,)), dma((ITERS + 1,)), dma((ITERS,)), dma((ITERS,)), dma, dma,
            dma((2, 2, 4)), dma((2, 2, 4)), dma((2,)), dma((2,)),
        ],
        compiler_params=pltpu.CompilerParams(
            collective_id=0, has_side_effects=True, vmem_limit_bytes=40 * 2**20
        ),
        name="coupling",
    )(noise, data)
    return (targets, noise_pot[0], data_pot[0])


def solution(mesh):
    placed = (P("row", "col"), P("col", "row"))
    return jax.shard_map(
        per_device,
        mesh=mesh,
        in_specs=placed,
        out_specs=(P(("row", "col"), None), P("row"), P("col")),
        check_vma=False,
    )
```

```python
import math

import jax
import jax.numpy as jnp
from jax import lax
from jax.experimental import pallas as pl
from jax.experimental.pallas import tpu as pltpu
from jax.sharding import PartitionSpec as P

LATENT = 16384
ITERS = 3
X, Y, Z = 4, 8, 8
N_ROW, N_COL = X * Y, 2 * Z
ROWS, COLS = 128, 256
LOG_COUNT = math.log(4096)
EPSILON = 0.64 / math.sqrt(LATENT)
BLOCK = 512
CHUNKS = 4
CHUNK = 256 // CHUNKS
MESH = pl.DeviceIdType.MESH
F32, BF16 = jnp.float32, jnp.bfloat16


def flip(line, copies):
    return jnp.transpose(jnp.broadcast_to(line, (copies, line.shape[1])))


def squares(block):
    block = jnp.square(block.astype(F32))
    return sum(block[:, i : i + 128] for i in range(0, block.shape[1], 128))


def hops(way, half):
    return 4 if way == half else 3


def legs(way, chunk):
    return hops(way, chunk // (CHUNKS // 2))


def kernel(
    noise_hbm, data_hbm, out_ref, noise_pot_ref, data_pot_ref,
    noise_ref, in_sem, nb, dd, part, part_in, square_sum, norm_slots, score, score_t, f_slots, g_slots,
    w_send, w_all, scales, po, rs_in, rs_out, fin_send, fin_in,
    own_send, own_recv, ring_send, ring_recv, pair_send, pair_recv, dpair_send, dpair_recv,
    part_s, part_r, norm_s, norm_r, f_send, f_recv, g_send, g_recv, w_s, w_r, sc_s, sc_r,
    rs_s, rs_r, fin_s, fin_r,
):
    row, col = lax.axis_index("row"), lax.axis_index("col")
    y, x = row // X, lax.rem(row, X)
    z, c = col // 2, lax.rem(col, 2)
    other = 1 - c

    def at(y_, x_, z_, c_):
        return (y_ * X + x_, z_ * 2 + c_)

    def wrap(i, n):
        return lax.rem(i + n, n)

    def send(src, dst, send_sem, recv_sem, device):
        return pltpu.make_async_remote_copy(
            src_ref=src, dst_ref=dst, send_sem=send_sem, recv_sem=recv_sem,
            device_id=device, device_id_type=MESH,
        )

    def take(ref, sem):
        pltpu.make_async_copy(ref, ref, sem).wait()

    drains = []
    barrier = pltpu.get_barrier_semaphore()
    near = [at(wrap(y + 1, Y), x, z, c), at(wrap(y - 1, Y), x, z, c)]
    near += [at(y, x, wrap(z + 1, Z), c), at(y, x, wrap(z - 1, Z), c), at(y, x, z, other)]
    for k in range(1, X):
        near += [at(y, wrap(x + k, X), z, c), at(y, wrap(x + k, X), z, other)]
    for device in near:
        pl.semaphore_signal(barrier, inc=1, device_id=device, device_id_type=MESH)
    data_ref = dd.at[c, y]
    noise_in = pltpu.make_async_copy(noise_hbm, noise_ref, in_sem.at[0])
    data_in = pltpu.make_async_copy(data_hbm, data_ref, in_sem.at[1])
    noise_in.start()
    data_in.start()
    part[...] = jnp.zeros_like(part)
    noise_in.wait()
    data_in.wait()
    pl.semaphore_wait(barrier, len(near))

    mine = x // 2 == c
    first = jnp.where(mine, lax.rem(x, 2), 1 - lax.rem(x, 2))

    def noise_chunk(block, core, chunk):
        half, rest = chunk // (CHUNKS // 2), chunk % (CHUNKS // 2)
        begin = core * 256 + jnp.where(first == half, 0, 1) * 128 + rest * CHUNK
        return nb.at[block, pl.ds(pl.multiple_of(begin, CHUNK), CHUNK)]

    def ring(kind, way, chunk, step):
        place = (y, z)[kind]
        sign = 1 - 2 * way
        block = wrap(place - sign * (step - 1), 8)
        target = wrap(place + sign, 8)
        if kind == 0:
            ref = dd.at[c, block, pl.ds(chunk * CHUNK, CHUNK)]
            device = at(target, x, z, c)
        else:
            ref = noise_chunk(block, c, chunk)
            device = at(y, x, target, c)
        index = (kind, way, chunk, step - 1)
        return send(ref, ref, ring_send.at[index], ring_recv.at[index], device)

    n1_device = [at(y, 2 * c + h, z, x // 2) for h in range(2)]
    n1_self = [jnp.logical_and(mine, lax.rem(x, 2) == h) for h in range(2)]
    n1 = []
    for rest in range(CHUNKS // 2):
        for h in range(2):
            src = noise_ref.at[pl.ds(rest * CHUNK, CHUNK), pl.ds(h * BLOCK, BLOCK)]
            dst = nb.at[z, pl.ds(pl.multiple_of(x * ROWS + rest * CHUNK, CHUNK), CHUNK)]
            sem = own_recv.at[lax.rem(x, 2), rest]
            far = send(src, dst, own_send.at[h, rest], sem, n1_device[h])
            near_copy = pltpu.make_async_copy(src, dst, sem)
            n1.append((h, far))

            @pl.when(n1_self[h])
            def _():
                near_copy.start()

            @pl.when(jnp.logical_not(n1_self[h]))
            def _():
                far.start()

    for chunk in range(CHUNKS):
        for way in range(2):
            ring(0, way, chunk, 1).start()

    def pair(way, chunk, step, block):
        index = (way, chunk, step)
        ref = noise_chunk(block, c, chunk)
        return send(ref, ref, pair_send.at[index], pair_recv.at[index], at(y, x, z, other))

    pairs = []
    for chunk in range(CHUNKS):
        half, rest = chunk // (CHUNKS // 2), chunk % (CHUNKS // 2)
        parity = jnp.where(first == half, 0, 1)
        take(noise_chunk(z, c, chunk), own_recv.at[parity, rest])
        for way in range(2):
            ring(1, way, chunk, 1).start()
        pairs.append(pair(0, chunk, 0, z))
        pairs[-1].start()

    square_sum[...] = squares(data_ref[...])
    last_data, last_noise = wrap(y + 4, Y), wrap(z + 4, Z)

    def product(a, b):
        return lax.dot_general(a, b, (((1,), (1,)), ((), ())), preferred_element_type=F32)

    for step in range(1, 5):
        for chunk in range(CHUNKS):
            for kind in range(2):
                for way in range(2):
                    if step > legs(way, chunk):
                        continue
                    ring(kind, way, chunk, step).wait_recv()
                    if step < legs(way, chunk):
                        ring(kind, way, chunk, step + 1).start()
                    if kind == 1:
                        block = wrap(z - (1 - 2 * way) * step, Z)
                        pairs.append(pair(way, chunk, step, block))
                        pairs[-1].start()
        if step < 4:
            for block in (wrap(y - step, Y), wrap(y + step, Y)):
                square_sum[...] += squares(dd[c, block])
        if step == 3:
            for copy in pairs:
                copy.wait_recv()
            early = len(pairs)

            @pl.loop(0, Y)
            def _(k):
                @pl.when(jnp.logical_and(k != last_data, k != last_noise))
                def _():
                    part[...] += product(nb[k], dd[c, k])
    for copy in pairs[early:]:
        copy.wait_recv()

    def drain_rings():
        for h, far in n1:
            @pl.when(jnp.logical_not(n1_self[h]))
            def _():
                far.wait_send()
        for kind in range(2):
            for chunk in range(CHUNKS):
                for way in range(2):
                    for step in range(1, legs(way, chunk) + 1):
                        ring(kind, way, chunk, step).wait_send()
        for copy in pairs:
            copy.wait_send()
    drains.append(drain_rings)
    part_copies = []
    for k in (2, 1, 3, 0):
        target = wrap(x + k, X)
        rows = pl.ds(pl.multiple_of(target * ROWS, ROWS), ROWS)
        part[rows, :] += product(nb[last_data, rows, :], dd[c, last_data])

        @pl.when(last_data != last_noise)
        def _():
            part[rows, :] += product(nb[last_noise, rows, :], dd[c, last_noise])

        if k:
            copy = send(
                part.at[rows], part_in.at[k - 1], part_s.at[k - 1], part_r.at[k - 1],
                at(y, target, z, c),
            )
            copy.start()
            part_copies.append(copy)
    square_sum[...] += squares(dd[c, wrap(y + 4, Y)])
    norm_slots[x] = jnp.sum(jnp.transpose(square_sum[...]), axis=0, keepdims=True)
    for k in range(1, X):
        send(
            norm_slots.at[x], norm_slots.at[x], norm_s, norm_r, at(y, wrap(x + k, X), z, c)
        ).start()
    fold = squares(noise_ref[...])
    noise_squares = jnp.sum(jnp.transpose(fold), axis=0, keepdims=True)
    for copy in part_copies:
        copy.wait_recv()
    total = part[pl.ds(pl.multiple_of(x * ROWS, ROWS), ROWS), :]
    total = total + part_in[0] + part_in[1] + part_in[2]
    score[...] = total * (2.0 / LATENT / EPSILON)
    score_t[...] = jnp.transpose(score[...])
    take(norm_slots.at[pl.ds(0, X - 1)], norm_r)
    data_norm = (norm_slots[0] + norm_slots[1] + norm_slots[2] + norm_slots[3]) / LATENT

    def drain_parts():
        for copy in part_copies:
            copy.wait_send()
        take(norm_slots.at[pl.ds(0, X - 1)], norm_s)
    drains.append(drain_parts)
    dpair = send(dd.at[c], dd.at[c], dpair_send, dpair_recv, at(y, x, z, other))
    dpair.start()

    def far_first(i, n):
        return n // 2 + (1 - 2 * lax.rem(i, 2)) * ((i + 1) // 2)

    def along_col(k):
        i = (k - 1) // 2
        return at(y, x, wrap(z + far_first(i, Z), Z), wrap(c + lax.rem(k, 2), 2))

    def along_row(k):
        i, j = (k - 1) // X, lax.rem(k - 1, X)
        return at(wrap(y + far_first(i, Y), Y), wrap(x + far_first(j, X), X), z, c)

    def post(scores, slots, step, me, count, target, send_sem, recv_sem):
        peak = jnp.max(scores, axis=0, keepdims=True)
        slots[step, me, 0:1, :] = peak
        slots[step, me, 1:2, :] = jnp.sum(jnp.exp(scores - peak), axis=0, keepdims=True)

        @pl.loop(1, count)
        def _(k):
            ref = slots.at[step, me]
            send(ref, ref, send_sem.at[step], recv_sem.at[step], target(k)).start()

        return peak

    def merge(slots, step, count, recv_sem):
        take(slots.at[step, pl.ds(0, count - 1)], recv_sem.at[step])
        peaks, sums = slots[step, :, 0, :], slots[step, :, 1, :]
        peak = jnp.max(peaks, axis=0, keepdims=True)
        total = jnp.sum(sums * jnp.exp(peaks - peak), axis=0, keepdims=True)
        return -(LOG_COUNT + peak + jnp.log(total))

    def wide(u):
        tile = flip(u, 128)
        return jnp.concatenate([tile] * (COLS // 128), axis=1)

    def post_noise(step, v):
        f_slots[step, col, 2:3, :] = noise_squares
        scores = score_t[...] + flip(v, ROWS)
        return post(scores, f_slots, step, col, N_COL, along_col, f_send, f_recv)

    def post_data(step, u):
        scores = score[...] + wide(u)
        return post(scores, g_slots, step, row, N_ROW, along_row, g_send, g_recv)

    v = -data_norm / EPSILON
    for step in range(ITERS):
        post_noise(step, v)
        u = merge(f_slots, step, N_COL, f_recv)
        post_data(step, u)
        v = merge(g_slots, step, N_ROW, g_recv)
    peak = post_noise(ITERS, v)

    def to_group(src, dst, send_sem, recv_sem):
        for k in (2, 1, 3, 0):
            for flipped in (1, 0):
                if k == 0 and flipped == 0:
                    continue
                core = wrap(c + flipped, 2)
                send(src(core), dst, send_sem, recv_sem, at(y, wrap(x + k, X), z, core)).start()

    member = c * X + x
    raw = jnp.exp(score[...] + v - wide(peak)).reshape(Z, 2, 8, COLS)
    for core in range(2):
        w_send[core] = raw[:, core].reshape(Z * 8, COLS).astype(BF16)
    to_group(lambda core: w_send.at[core], w_all.at[member], w_s, w_r)
    w_all[member] = w_send[c]
    u = merge(f_slots, ITERS, N_COL, f_recv)
    scales[member] = jnp.exp(u + peak + LOG_COUNT)
    to_group(lambda core: scales.at[member], scales.at[member], sc_s, sc_r)
    noise_norm = jnp.sum(f_slots[0, :, 2, :], axis=0, keepdims=True) / LATENT
    noise_pot_ref[...] = EPSILON * u + noise_norm
    data_pot_ref[...] = EPSILON * v + data_norm
    dpair.wait_recv()

    def drain_sink():
        for step in range(ITERS + 1):
            take(f_slots.at[step, pl.ds(0, N_COL - 1)], f_send.at[step])
        for step in range(ITERS):
            take(g_slots.at[step, pl.ds(0, N_ROW - 1)], g_send.at[step])
    drains.append(drain_sink)
    drains.append(dpair.wait_send)
    take(w_all.at[pl.ds(0, 2 * X - 1)], w_r)
    take(scales.at[pl.ds(0, 2 * X - 1)], sc_r)
    factors = jnp.transpose(scales[:, 0, :]).reshape(Z, 2, 8, 2 * X)
    factors = jnp.where(c == 0, factors[:, 0], factors[:, 1]).reshape(Z * 8, 2 * X)
    for k in range(2 * X):
        w_all[k] = (w_all[k].astype(F32) * factors[:, k : k + 1]).astype(BF16)
    drains.append(lambda: take(w_all.at[pl.ds(0, 2 * X - 1)], w_s))
    drains.append(lambda: take(scales.at[pl.ds(0, 2 * X - 1)], sc_s))
    def rs(way, half, step):
        sign = 1 - 2 * way
        index = (way, half, step - 1)
        if step == 1:
            src = po.at[half, wrap(z + sign * hops(way, half), Z)]
        else:
            src = rs_out.at[way, half, step - 2]
        return send(
            src, rs_in.at[index], rs_s.at[index], rs_r.at[index], at(y, x, wrap(z + sign, Z), c)
        )

    for half in range(2):
        @pl.loop(0, Y // 2)
        def _(j):
            block = half * (Y // 2) + j
            sums = jnp.dot(
                w_all[0:X].reshape(256, COLS), dd[0, block], preferred_element_type=F32
            ) + jnp.dot(w_all[X:].reshape(256, COLS), dd[1, block], preferred_element_type=F32)
            sums = sums.reshape(X, Z, 8, BLOCK)
            columns = pl.ds(pl.multiple_of(j * BLOCK, BLOCK), BLOCK)
            for k in range(Z):
                po[half, k, :, columns] = sums[:, k].reshape(X * 8, BLOCK).astype(BF16)

        for way in range(2):
            rs(way, half, 1).start()

    def finish(half):
        sums = po[half, z].astype(F32)
        for way in range(2):
            sums = sums + rs_in[way, half, hops(way, half) - 1].astype(F32)
        for k in range(X):
            lines = sums[k * 8 : k * 8 + 8]
            lines = jnp.concatenate([lines[:, :1024], lines[:, 1024:]], axis=0)
            fin_send[half, k] = lines.astype(BF16)
        for k in (2, 1, 3):
            target = wrap(x + k, X)
            send(
                fin_send.at[half, target], fin_in.at[half, x], fin_s.at[half], fin_r.at[half],
                at(y, target, z, c),
            ).start()
        fin_in[half, x] = fin_send[half, x]

    for step in range(1, 5):
        for half in range(2):
            for way in range(2):
                if step > hops(way, half):
                    continue
                rs(way, half, step).wait_recv()
                if step < hops(way, half):
                    target = wrap(z + (1 - 2 * way) * (hops(way, half) - step), Z)
                    rs_out[way, half, step - 1] = (
                        rs_in[way, half, step - 1].astype(F32) + po[half, target].astype(F32)
                    ).astype(BF16)
                    rs(way, half, step + 1).start()
            if step == 4:
                finish(half)

    def drain_rs():
        for half in range(2):
            for way in range(2):
                for step in range(1, hops(way, half) + 1):
                    rs(way, half, step).wait_send()
    drains.append(drain_rs)
    for half in range(2):
        take(fin_in.at[half, pl.ds(0, X - 1)], fin_r.at[half])
        for k in range(X):
            lines = fin_in[half, k].astype(F32)
            for quarter in range(2):
                for part_block in range(2):
                    block = half * 4 + quarter * 2 + part_block
                    begin = (block * X + k) * BLOCK
                    out_ref[:, begin : begin + BLOCK] = lines[
                        quarter * 8 : quarter * 8 + 8, part_block * BLOCK : (part_block + 1) * BLOCK
                    ].astype(BF16)

    def drain_fin():
        for half in range(2):
            take(fin_in.at[half, pl.ds(0, X - 1)], fin_s.at[half])
    drains.append(drain_fin)
    for d in drains:
        d()


def per_device(noise, data):
    vmem = pl.BlockSpec(memory_space=pltpu.VMEM)
    dma = pltpu.SemaphoreType.DMA
    targets, noise_pot, data_pot = pl.pallas_call(
        kernel,
        out_shape=(
            jax.ShapeDtypeStruct((8, LATENT), BF16),
            jax.ShapeDtypeStruct((1, ROWS), F32),
            jax.ShapeDtypeStruct((1, COLS), F32),
        ),
        in_specs=[pl.BlockSpec(memory_space=pltpu.HBM)] * 2,
        out_specs=(vmem, vmem, vmem),
        scratch_shapes=[
            pltpu.VMEM((ROWS, 1024), BF16), dma((2,)),
            pltpu.VMEM((Z, X * ROWS, BLOCK), BF16),
            pltpu.VMEM((2, Y, COLS, BLOCK), BF16),
            pltpu.VMEM((X * ROWS, COLS), F32),
            pltpu.VMEM((X - 1, ROWS, COLS), F32),
            pltpu.VMEM((COLS, 128), F32),
            pltpu.VMEM((X, 1, COLS), F32),
            pltpu.VMEM((ROWS, COLS), F32),
            pltpu.VMEM((COLS, ROWS), F32),
            pltpu.VMEM((ITERS + 1, N_COL, 3, ROWS), F32),
            pltpu.VMEM((ITERS, N_ROW, 2, COLS), F32),
            pltpu.VMEM((2, Z * 8, COLS), BF16),
            pltpu.VMEM((2 * X, Z * 8, COLS), BF16),
            pltpu.VMEM((2 * X, 1, ROWS), F32),
            pltpu.VMEM((2, Z, X * 8, 2048), BF16),
            pltpu.VMEM((2, 2, 4, X * 8, 2048), BF16),
            pltpu.VMEM((2, 2, 3, X * 8, 2048), BF16),
            pltpu.VMEM((2, X, 16, 1024), BF16),
            pltpu.VMEM((2, X, 16, 1024), BF16),
            dma((2, CHUNKS // 2)), dma((2, CHUNKS // 2)),
            dma((2, 2, CHUNKS, 4)), dma((2, 2, CHUNKS, 4)),
            dma((2, CHUNKS, 5)), dma((2, CHUNKS, 5)), dma, dma,
            dma((3,)), dma((3,)), dma, dma,
            dma((ITERS + 1,)), dma((ITERS + 1,)), dma((ITERS,)), dma((ITERS,)), dma, dma, dma, dma,
            dma((2, 2, 4)), dma((2, 2, 4)), dma((2,)), dma((2,)),
        ],
        compiler_params=pltpu.CompilerParams(
            collective_id=0, has_side_effects=True, vmem_limit_bytes=60 * 2**20
        ),
        name="coupling",
    )(noise, data)
    return (targets, noise_pot[0], data_pot[0])


def solution(mesh):
    placed = (P("row", "col"), P("col", "row"))
    return jax.shard_map(
        per_device,
        mesh=mesh,
        in_specs=placed,
        out_specs=(P(("row", "col"), None), P("row"), P("col")),
        check_vma=False,
    )
```

```python
import functools
import math

import jax
import jax.numpy as jnp
from jax import lax
from jax.experimental import pallas as pl
from jax.experimental.pallas import tpu as pltpu
from jax.sharding import PartitionSpec as P

LATENT = 16384
ITERS = 3
X, Y, Z = 4, 8, 8
N_ROW, N_COL = X * Y, 2 * Z
ROWS, COLS = 128, 256
LOG_COUNT = math.log(4096)
EPSILON = 0.64 / math.sqrt(LATENT)
BLOCK = 512
CHUNKS = 4
CHUNK = 256 // CHUNKS
MESH = pl.DeviceIdType.MESH
F32, BF16 = jnp.float32, jnp.bfloat16


def flip(line, copies):
    return jnp.transpose(jnp.broadcast_to(line, (copies, line.shape[1])))


def squares(block):
    block = jnp.square(block.astype(F32))
    return sum(block[:, i : i + 128] for i in range(0, block.shape[1], 128))


def hops(way, half):
    return 4 if way == half else 3


def legs(way, chunk):
    return hops(way, chunk // (CHUNKS // 2))


def kernel(
    noise_hbm, data_hbm, out_ref, noise_pot_ref, data_pot_ref,
    noise_ref, in_sem, nb, dd, part, part_in, square_sum, norm_slots, score, score_t, f_slots, g_slots,
    w_send, w_all, h_slots, po, rs_in, rs_out, fin_send, fin_in,
    own_send, own_recv, ring_send, ring_recv, pair_send, pair_recv, dpair_send, dpair_recv,
    part_s, part_r, norm_s, norm_r, f_send, f_recv, g_send, g_recv, w_s, w_r, h_send, h_recv,
    rs_s, rs_r, fin_s, fin_r,
):
    row, col = lax.axis_index("row"), lax.axis_index("col")
    y, x = row // X, lax.rem(row, X)
    z, c = col // 2, lax.rem(col, 2)
    other = 1 - c

    def at(y_, x_, z_, c_):
        return (y_ * X + x_, z_ * 2 + c_)

    def wrap(i, n):
        return lax.rem(i + n, n)

    def send(src, dst, send_sem, recv_sem, device):
        return pltpu.make_async_remote_copy(
            src_ref=src, dst_ref=dst, send_sem=send_sem, recv_sem=recv_sem,
            device_id=device, device_id_type=MESH,
        )

    def take(ref, sem):
        pltpu.make_async_copy(ref, ref, sem).wait()

    drains = []

    def flush():
        while drains:
            drains.pop(0)()

    barrier = pltpu.get_barrier_semaphore()
    near = [at(wrap(y + 1, Y), x, z, c), at(wrap(y - 1, Y), x, z, c)]
    near += [at(y, x, wrap(z + 1, Z), c), at(y, x, wrap(z - 1, Z), c), at(y, x, z, other)]
    for k in range(1, X):
        near += [at(y, wrap(x + k, X), z, c), at(y, wrap(x + k, X), z, other)]
    for device in near:
        pl.semaphore_signal(barrier, inc=1, device_id=device, device_id_type=MESH)
    data_ref = dd.at[c, y]
    noise_in = pltpu.make_async_copy(noise_hbm, noise_ref, in_sem.at[0])
    data_in = pltpu.make_async_copy(data_hbm, data_ref, in_sem.at[1])
    noise_in.start()
    data_in.start()
    part[...] = jnp.zeros_like(part)
    noise_in.wait()
    data_in.wait()
    pl.semaphore_wait(barrier, len(near))

    mine = x // 2 == c
    first = jnp.where(mine, lax.rem(x, 2), 1 - lax.rem(x, 2))

    def noise_chunk(block, core, chunk):
        half, rest = chunk // (CHUNKS // 2), chunk % (CHUNKS // 2)
        begin = core * 256 + jnp.where(first == half, 0, 1) * 128 + rest * CHUNK
        return nb.at[block, pl.ds(pl.multiple_of(begin, CHUNK), CHUNK)]

    def ring(kind, way, chunk, step):
        place = (y, z)[kind]
        sign = 1 - 2 * way
        block = wrap(place - sign * (step - 1), 8)
        target = wrap(place + sign, 8)
        if kind == 0:
            ref = dd.at[c, block, pl.ds(chunk * CHUNK, CHUNK)]
            device = at(target, x, z, c)
        else:
            ref = noise_chunk(block, c, chunk)
            device = at(y, x, target, c)
        index = (kind, way, chunk, step - 1)
        return send(ref, ref, ring_send.at[kind], ring_recv.at[index], device)

    n1_device = [at(y, 2 * c + h, z, x // 2) for h in range(2)]
    n1_self = [jnp.logical_and(mine, lax.rem(x, 2) == h) for h in range(2)]
    n1 = []
    for rest in range(CHUNKS // 2):
        for h in range(2):
            src = noise_ref.at[pl.ds(rest * CHUNK, CHUNK), pl.ds(h * BLOCK, BLOCK)]
            dst = nb.at[z, pl.ds(pl.multiple_of(x * ROWS + rest * CHUNK, CHUNK), CHUNK)]
            sem = own_recv.at[lax.rem(x, 2), rest]
            far = send(src, dst, own_send.at[h, rest], sem, n1_device[h])
            near_copy = pltpu.make_async_copy(src, dst, sem)
            n1.append((h, far))

            @pl.when(n1_self[h])
            def _():
                near_copy.start()

            @pl.when(jnp.logical_not(n1_self[h]))
            def _():
                far.start()

    for chunk in range(CHUNKS):
        for way in range(2):
            ring(0, way, chunk, 1).start()

    def pair(way, chunk, step, block):
        index = (way, chunk, step)
        ref = noise_chunk(block, c, chunk)
        return send(ref, ref, pair_send, pair_recv.at[index], at(y, x, z, other))

    pairs = []
    for chunk in range(CHUNKS):
        half, rest = chunk // (CHUNKS // 2), chunk % (CHUNKS // 2)
        parity = jnp.where(first == half, 0, 1)
        take(noise_chunk(z, c, chunk), own_recv.at[parity, rest])
        for way in range(2):
            ring(1, way, chunk, 1).start()
        pairs.append(pair(0, chunk, 0, z))
        pairs[-1].start()

    square_sum[...] = squares(data_ref[...])
    last_data, last_noise = wrap(y + 4, Y), wrap(z + 4, Z)

    def product(a, b):
        return lax.dot_general(a, b, (((1,), (1,)), ((), ())), preferred_element_type=F32)

    for step in range(1, 5):
        for chunk in range(CHUNKS):
            for kind in range(2):
                for way in range(2):
                    if step > legs(way, chunk):
                        continue
                    ring(kind, way, chunk, step).wait_recv()
                    if step < legs(way, chunk):
                        ring(kind, way, chunk, step + 1).start()
                    if kind == 1:
                        block = wrap(z - (1 - 2 * way) * step, Z)
                        pairs.append(pair(way, chunk, step, block))
                        pairs[-1].start()
        if step < 4:
            for block in (wrap(y - step, Y), wrap(y + step, Y)):
                square_sum[...] += squares(dd[c, block])
        if step == 3:
            for copy in pairs:
                copy.wait_recv()
            early = len(pairs)

            @pl.loop(0, Y)
            def _(k):
                @pl.when(jnp.logical_and(k != last_data, k != last_noise))
                def _():
                    part[...] += product(nb[k], dd[c, k])
    for copy in pairs[early:]:
        copy.wait_recv()

    def drain_rings():
        for h, far in n1:
            @pl.when(jnp.logical_not(n1_self[h]))
            def _():
                far.wait_send()
        take(dd.at[c, pl.ds(0, Y - 1)], ring_send.at[0])
        take(nb.at[pl.ds(0, Z - 1), pl.ds(0, 256)], ring_send.at[1])
        take(nb.at[:, pl.ds(0, 256)], pair_send)
    drains.append(drain_rings)
    part_copies = []
    for k in (2, 1, 3, 0):
        target = wrap(x + k, X)
        rows = pl.ds(pl.multiple_of(target * ROWS, ROWS), ROWS)
        part[rows, :] += product(nb[last_data, rows, :], dd[c, last_data])

        @pl.when(last_data != last_noise)
        def _():
            part[rows, :] += product(nb[last_noise, rows, :], dd[c, last_noise])

        if k:
            copy = send(
                part.at[rows], part_in.at[k - 1], part_s.at[k - 1], part_r.at[k - 1],
                at(y, target, z, c),
            )
            copy.start()
            part_copies.append(copy)
    square_sum[...] += squares(dd[c, wrap(y + 4, Y)])
    norm_slots[x] = jnp.sum(jnp.transpose(square_sum[...]), axis=0, keepdims=True)
    for k in range(1, X):
        send(
            norm_slots.at[x], norm_slots.at[x], norm_s, norm_r, at(y, wrap(x + k, X), z, c)
        ).start()
    fold = squares(noise_ref[...])
    noise_squares = jnp.sum(jnp.transpose(fold), axis=0, keepdims=True)
    for copy in part_copies:
        copy.wait_recv()
    total = part[pl.ds(pl.multiple_of(x * ROWS, ROWS), ROWS), :]
    total = total + part_in[0] + part_in[1] + part_in[2]
    score[...] = total * (2.0 / LATENT / EPSILON)
    score_t[...] = jnp.transpose(score[...])
    take(norm_slots.at[pl.ds(0, X - 1)], norm_r)
    data_norm = (norm_slots[0] + norm_slots[1] + norm_slots[2] + norm_slots[3]) / LATENT

    def drain_parts():
        for copy in part_copies:
            copy.wait_send()
        take(norm_slots.at[pl.ds(0, X - 1)], norm_s)
    drains.append(drain_parts)
    dpair = send(dd.at[c], dd.at[c], dpair_send, dpair_recv, at(y, x, z, other))

    def far_first(i, n):
        return n // 2 + (1 - 2 * lax.rem(i, 2)) * ((i + 1) // 2)

    def along_col(k):
        i = (k - 1) // 2
        return at(y, x, wrap(z + far_first(i, Z), Z), wrap(c + lax.rem(k, 2), 2))

    def along_both(k):
        i, j = (k - 1) // (2 * X), lax.rem((k - 1) // 2, X)
        z_, x_ = wrap(z + far_first(i, Z), Z), wrap(x + far_first(j, X), X)
        return at(y, x_, z_, wrap(c + lax.rem(k, 2), 2))

    def along_row(k):
        i, j = (k - 1) // X, lax.rem(k - 1, X)
        return at(wrap(y + far_first(i, Y), Y), wrap(x + far_first(j, X), X), z, c)

    def post(scores, slots, step, me, count, target, send_sem, recv_sem):
        peak = jnp.max(scores, axis=0, keepdims=True)
        slots[step, me, 0:1, :] = peak
        slots[step, me, 1:2, :] = jnp.sum(jnp.exp(scores - peak), axis=0, keepdims=True)

        @pl.loop(1, count)
        def _(k):
            ref = slots.at[step, me]
            send(ref, ref, send_sem.at[step], recv_sem.at[step], target(k)).start()

        return peak

    def merge(slots, step, count, recv_sem):
        take(slots.at[step, pl.ds(0, count - 1)], recv_sem.at[step])
        return combine(slots[step])

    def drain(slots, step, count, send_sem):
        take(slots.at[step, pl.ds(0, count - 1)], send_sem.at[step])

    def combine(slots):
        peaks, sums = slots[:, 0, :], slots[:, 1, :]
        peak = jnp.max(peaks, axis=0, keepdims=True)
        total = jnp.sum(sums * jnp.exp(peaks - peak), axis=0, keepdims=True)
        return -(LOG_COUNT + peak + jnp.log(total))

    def wide(u):
        tile = flip(u, 128)
        return jnp.concatenate([tile] * (COLS // 128), axis=1)

    def post_noise(step, v):
        f_slots[step, col, 2:3, :] = noise_squares
        scores = score_t[...] + flip(v, ROWS)
        return post(scores, f_slots, step, col, N_COL, along_col, f_send, f_recv)

    def post_data(step, u):
        scores = score[...] + wide(u)
        return post(scores, g_slots, step, row, N_ROW, along_row, g_send, g_recv)

    v = -data_norm / EPSILON
    for step in range(ITERS):
        post_noise(step, v)
        flush()
        drains.append(functools.partial(drain, f_slots, step, N_COL, f_send))
        u = merge(f_slots, step, N_COL, f_recv)
        post_data(step, u)
        if step == 0:
            dpair.start()
        flush()
        drains.append(functools.partial(drain, g_slots, step, N_ROW, g_send))
        v = merge(g_slots, step, N_ROW, g_recv)
    scores = score_t[...] + flip(v, ROWS)
    peak = post(scores, h_slots, 0, x * N_COL + col, X * N_COL, along_both, h_send, h_recv)
    flush()

    def to_group(src, dst, send_sem, recv_sem):
        for k in (2, 1, 3, 0):
            for flipped in (1, 0):
                if k == 0 and flipped == 0:
                    continue
                core = wrap(c + flipped, 2)
                send(src(core), dst, send_sem, recv_sem, at(y, wrap(x + k, X), z, core)).start()

    member = c * X + x
    raw = jnp.exp(score[...] + v - wide(peak)).reshape(Z, 2, 8, COLS)
    for core in range(2):
        w_send[core] = raw[:, core].reshape(Z * 8, COLS).astype(BF16)
    to_group(lambda core: w_send.at[core], w_all.at[member], w_s, w_r)
    w_all[member] = w_send[c]
    drains.append(lambda: take(h_slots.at[0, pl.ds(0, X * N_COL - 1)], h_send.at[0]))
    take(h_slots.at[0, pl.ds(0, X * N_COL - 1)], h_recv.at[0])
    us, factors = [], [None] * (2 * X)
    for k in range(X):
        us.append(combine(h_slots[0, pl.ds(k * N_COL, N_COL)]))
        for core in range(2):
            source = h_slots[0, k * N_COL + z * 2 + core]
            factors[core * X + k] = jnp.exp(us[k] + source[0:1, :] + LOG_COUNT)
    u = us[0]
    for k in range(1, X):
        u = jnp.where(x == k, us[k], u)
    noise_norm = jnp.sum(f_slots[0, :, 2, :], axis=0, keepdims=True) / LATENT
    noise_pot_ref[...] = EPSILON * u + noise_norm
    data_pot_ref[...] = EPSILON * v + data_norm
    dpair.wait_recv()

    drains.append(dpair.wait_send)
    take(w_all.at[pl.ds(0, 2 * X - 1)], w_r)
    factors = jnp.transpose(jnp.concatenate(factors, axis=0)).reshape(Z, 2, 8, 2 * X)
    factors = jnp.where(c == 0, factors[:, 0], factors[:, 1]).reshape(Z * 8, 2 * X)
    for k in range(2 * X):
        w_all[k] = (w_all[k].astype(F32) * factors[:, k : k + 1]).astype(BF16)
    drains.append(lambda: take(w_all.at[pl.ds(0, 2 * X - 1)], w_s))
    def rs(way, half, step):
        sign = 1 - 2 * way
        index = (way, half, step - 1)
        if step == 1:
            src = po.at[half, wrap(z + sign * hops(way, half), Z)]
        else:
            src = rs_out.at[way, half, step - 2]
        return send(
            src, rs_in.at[index], rs_s.at[index], rs_r.at[index], at(y, x, wrap(z + sign, Z), c)
        )

    for half in range(2):
        @pl.loop(0, Y // 2)
        def _(j):
            block = half * (Y // 2) + j
            sums = jnp.dot(
                w_all[0:X].reshape(256, COLS), dd[0, block], preferred_element_type=F32
            ) + jnp.dot(w_all[X:].reshape(256, COLS), dd[1, block], preferred_element_type=F32)
            sums = sums.reshape(X, Z, 8, BLOCK)
            columns = pl.ds(pl.multiple_of(j * BLOCK, BLOCK), BLOCK)
            for k in range(Z):
                po[half, k, :, columns] = sums[:, k].reshape(X * 8, BLOCK).astype(BF16)

        for way in range(2):
            rs(way, half, 1).start()

    def finish(half):
        sums = po[half, z].astype(F32)
        for way in range(2):
            sums = sums + rs_in[way, half, hops(way, half) - 1].astype(F32)
        for k in range(X):
            lines = sums[k * 8 : k * 8 + 8]
            lines = jnp.concatenate([lines[:, :1024], lines[:, 1024:]], axis=0)
            fin_send[half, k] = lines.astype(BF16)
        for k in (2, 1, 3):
            target = wrap(x + k, X)
            send(
                fin_send.at[half, target], fin_in.at[half, x], fin_s.at[half], fin_r.at[half],
                at(y, target, z, c),
            ).start()
        fin_in[half, x] = fin_send[half, x]

    flush()
    for step in range(1, 5):
        for half in range(2):
            for way in range(2):
                if step > hops(way, half):
                    continue
                rs(way, half, step).wait_recv()
                if step < hops(way, half):
                    target = wrap(z + (1 - 2 * way) * (hops(way, half) - step), Z)
                    rs_out[way, half, step - 1] = (
                        rs_in[way, half, step - 1].astype(F32) + po[half, target].astype(F32)
                    ).astype(BF16)
                    rs(way, half, step + 1).start()
            if step == 4:
                finish(half)

    def drain_rs():
        for half in range(2):
            for way in range(2):
                for step in range(1, hops(way, half) + 1):
                    rs(way, half, step).wait_send()
    drain_rs()
    for half in range(2):
        take(fin_in.at[half, pl.ds(0, X - 1)], fin_r.at[half])
        for k in range(X):
            lines = fin_in[half, k].astype(F32)
            for quarter in range(2):
                for part_block in range(2):
                    block = half * 4 + quarter * 2 + part_block
                    begin = (block * X + k) * BLOCK
                    out_ref[:, begin : begin + BLOCK] = lines[
                        quarter * 8 : quarter * 8 + 8, part_block * BLOCK : (part_block + 1) * BLOCK
                    ].astype(BF16)

    def drain_fin():
        for half in range(2):
            take(fin_in.at[half, pl.ds(0, X - 1)], fin_s.at[half])
    drains.append(drain_fin)
    flush()


def per_device(noise, data):
    vmem = pl.BlockSpec(memory_space=pltpu.VMEM)
    dma = pltpu.SemaphoreType.DMA
    targets, noise_pot, data_pot = pl.pallas_call(
        kernel,
        out_shape=(
            jax.ShapeDtypeStruct((8, LATENT), BF16),
            jax.ShapeDtypeStruct((1, ROWS), F32),
            jax.ShapeDtypeStruct((1, COLS), F32),
        ),
        in_specs=[pl.BlockSpec(memory_space=pltpu.HBM)] * 2,
        out_specs=(vmem, vmem, vmem),
        scratch_shapes=[
            pltpu.VMEM((ROWS, 1024), BF16), dma((2,)),
            pltpu.VMEM((Z, X * ROWS, BLOCK), BF16),
            pltpu.VMEM((2, Y, COLS, BLOCK), BF16),
            pltpu.VMEM((X * ROWS, COLS), F32),
            pltpu.VMEM((X - 1, ROWS, COLS), F32),
            pltpu.VMEM((COLS, 128), F32),
            pltpu.VMEM((X, 1, COLS), F32),
            pltpu.VMEM((ROWS, COLS), F32),
            pltpu.VMEM((COLS, ROWS), F32),
            pltpu.VMEM((ITERS, N_COL, 3, ROWS), F32),
            pltpu.VMEM((ITERS, N_ROW, 2, COLS), F32),
            pltpu.VMEM((2, Z * 8, COLS), BF16),
            pltpu.VMEM((2 * X, Z * 8, COLS), BF16),
            pltpu.VMEM((1, X * N_COL, 2, ROWS), F32),
            pltpu.VMEM((2, Z, X * 8, 2048), BF16),
            pltpu.VMEM((2, 2, 4, X * 8, 2048), BF16),
            pltpu.VMEM((2, 2, 3, X * 8, 2048), BF16),
            pltpu.VMEM((2, X, 16, 1024), BF16),
            pltpu.VMEM((2, X, 16, 1024), BF16),
            dma((2, CHUNKS // 2)), dma((2, CHUNKS // 2)),
            dma((2,)), dma((2, 2, CHUNKS, 4)),
            dma, dma((2, CHUNKS, 5)), dma, dma,
            dma((3,)), dma((3,)), dma, dma,
            dma((ITERS,)), dma((ITERS,)), dma((ITERS,)), dma((ITERS,)), dma, dma, dma((1,)), dma((1,)),
            dma((2, 2, 4)), dma((2, 2, 4)), dma((2,)), dma((2,)),
        ],
        compiler_params=pltpu.CompilerParams(
            collective_id=0, has_side_effects=True, vmem_limit_bytes=60 * 2**20
        ),
        name="coupling",
    )(noise, data)
    return (targets, noise_pot[0], data_pot[0])


def solution(mesh):
    placed = (P("row", "col"), P("col", "row"))
    return jax.shard_map(
        per_device,
        mesh=mesh,
        in_specs=placed,
        out_specs=(P(("row", "col"), None), P("row"), P("col")),
        check_vma=False,
    )
```

```python
import functools
import math

import jax
import jax.numpy as jnp
from jax import lax
from jax.experimental import pallas as pl
from jax.experimental.pallas import tpu as pltpu
from jax.sharding import PartitionSpec as P

LATENT = 16384
ITERS = 3
X, Y, Z = 4, 8, 8
N_ROW, N_COL = X * Y, 2 * Z
ROWS, COLS = 128, 256
LOG_COUNT = math.log(4096)
EPSILON = 0.64 / math.sqrt(LATENT)
BLOCK = 512
CHUNKS = 4
CHUNK = 256 // CHUNKS
PIECES = 4
PIECE = Y * BLOCK // PIECES
MESH = pl.DeviceIdType.MESH
F32, BF16 = jnp.float32, jnp.bfloat16


def flip(line, copies):
    return jnp.transpose(jnp.broadcast_to(line, (copies, line.shape[1])))


def squares(block):
    block = jnp.square(block.astype(F32))
    return sum(block[:, i : i + 128] for i in range(0, block.shape[1], 128))


def hops(way, half):
    return 4 if way == half else 3


def legs(way, chunk):
    return hops(way, chunk // (CHUNKS // 2))


def turns(way, piece):
    return hops(way, piece // (PIECES // 2))


def kernel(
    noise_hbm, data_hbm, out_ref, noise_pot_ref, data_pot_ref,
    noise_ref, in_sem, nb, dd, part, part_in, square_sum, norm_slots, score, score_t, f_slots, g_slots,
    w_send, w_all, h_slots, po, rs_in, rs_out, fin_send, fin_in,
    own_send, own_recv, ring_send, ring_recv, pair_send, pair_recv, dpair_send, dpair_recv,
    part_s, part_r, norm_s, norm_r, f_send, f_recv, g_send, g_recv, w_s, w_r, h_send, h_recv,
    rs_s, rs_r, fin_s, fin_r,
):
    row, col = lax.axis_index("row"), lax.axis_index("col")
    y, x = row // X, lax.rem(row, X)
    z, c = col // 2, lax.rem(col, 2)
    other = 1 - c

    def at(y_, x_, z_, c_):
        return (y_ * X + x_, z_ * 2 + c_)

    def wrap(i, n):
        return lax.rem(i + n, n)

    def send(src, dst, send_sem, recv_sem, device):
        return pltpu.make_async_remote_copy(
            src_ref=src, dst_ref=dst, send_sem=send_sem, recv_sem=recv_sem,
            device_id=device, device_id_type=MESH,
        )

    def take(ref, sem):
        pltpu.make_async_copy(ref, ref, sem).wait()

    drains = []

    def flush():
        while drains:
            drains.pop(0)()

    barrier = pltpu.get_barrier_semaphore()
    near = [at(wrap(y + 1, Y), x, z, c), at(wrap(y - 1, Y), x, z, c)]
    near += [at(y, x, wrap(z + 1, Z), c), at(y, x, wrap(z - 1, Z), c), at(y, x, z, other)]
    for k in range(1, X):
        near += [at(y, wrap(x + k, X), z, c), at(y, wrap(x + k, X), z, other)]
    for device in near:
        pl.semaphore_signal(barrier, inc=1, device_id=device, device_id_type=MESH)
    data_ref = dd.at[c, y]
    noise_in = pltpu.make_async_copy(noise_hbm, noise_ref, in_sem.at[0])
    data_in = pltpu.make_async_copy(data_hbm, data_ref, in_sem.at[1])
    noise_in.start()
    data_in.start()
    part[...] = jnp.zeros_like(part)
    noise_in.wait()
    data_in.wait()
    pl.semaphore_wait(barrier, len(near))

    mine = x // 2 == c
    first = jnp.where(mine, lax.rem(x, 2), 1 - lax.rem(x, 2))

    def noise_chunk(block, core, chunk):
        half, rest = chunk // (CHUNKS // 2), chunk % (CHUNKS // 2)
        begin = core * 256 + jnp.where(first == half, 0, 1) * 128 + rest * CHUNK
        return nb.at[block, pl.ds(pl.multiple_of(begin, CHUNK), CHUNK)]

    def ring(kind, way, chunk, step):
        place = (y, z)[kind]
        sign = 1 - 2 * way
        block = wrap(place - sign * (step - 1), 8)
        target = wrap(place + sign, 8)
        if kind == 0:
            ref = dd.at[c, block, pl.ds(chunk * CHUNK, CHUNK)]
            device = at(target, x, z, c)
        else:
            ref = noise_chunk(block, c, chunk)
            device = at(y, x, target, c)
        index = (kind, way, chunk, step - 1)
        return send(ref, ref, ring_send.at[kind], ring_recv.at[index], device)

    n1_device = [at(y, 2 * c + h, z, x // 2) for h in range(2)]
    n1_self = [jnp.logical_and(mine, lax.rem(x, 2) == h) for h in range(2)]
    n1 = []
    for rest in range(CHUNKS // 2):
        for h in range(2):
            src = noise_ref.at[pl.ds(rest * CHUNK, CHUNK), pl.ds(h * BLOCK, BLOCK)]
            dst = nb.at[z, pl.ds(pl.multiple_of(x * ROWS + rest * CHUNK, CHUNK), CHUNK)]
            sem = own_recv.at[lax.rem(x, 2), rest]
            far = send(src, dst, own_send.at[h, rest], sem, n1_device[h])
            near_copy = pltpu.make_async_copy(src, dst, sem)
            n1.append((h, far))

            @pl.when(n1_self[h])
            def _():
                near_copy.start()

            @pl.when(jnp.logical_not(n1_self[h]))
            def _():
                far.start()

    for chunk in range(CHUNKS):
        for way in range(2):
            ring(0, way, chunk, 1).start()

    def pair(way, chunk, step, block):
        index = (way, chunk, step)
        ref = noise_chunk(block, c, chunk)
        return send(ref, ref, pair_send, pair_recv.at[index], at(y, x, z, other))

    pairs = []
    for chunk in range(CHUNKS):
        half, rest = chunk // (CHUNKS // 2), chunk % (CHUNKS // 2)
        parity = jnp.where(first == half, 0, 1)
        take(noise_chunk(z, c, chunk), own_recv.at[parity, rest])
        for way in range(2):
            ring(1, way, chunk, 1).start()
        pairs.append(pair(0, chunk, 0, z))
        pairs[-1].start()

    square_sum[...] = squares(data_ref[...])
    last_data, last_noise = wrap(y + 4, Y), wrap(z + 4, Z)

    def product(a, b):
        return lax.dot_general(a, b, (((1,), (1,)), ((), ())), preferred_element_type=F32)

    for step in range(1, 5):
        for chunk in range(CHUNKS):
            for kind in range(2):
                for way in range(2):
                    if step > legs(way, chunk):
                        continue
                    ring(kind, way, chunk, step).wait_recv()
                    if step < legs(way, chunk):
                        ring(kind, way, chunk, step + 1).start()
                    if kind == 1:
                        block = wrap(z - (1 - 2 * way) * step, Z)
                        pairs.append(pair(way, chunk, step, block))
                        pairs[-1].start()
        if step < 4:
            for block in (wrap(y - step, Y), wrap(y + step, Y)):
                square_sum[...] += squares(dd[c, block])
        if step == 3:
            for copy in pairs:
                copy.wait_recv()
            early = len(pairs)

            @pl.loop(0, Y)
            def _(k):
                @pl.when(jnp.logical_and(k != last_data, k != last_noise))
                def _():
                    part[...] += product(nb[k], dd[c, k])
    for copy in pairs[early:]:
        copy.wait_recv()

    def drain_rings():
        for h, far in n1:
            @pl.when(jnp.logical_not(n1_self[h]))
            def _():
                far.wait_send()
        take(dd.at[c, pl.ds(0, Y - 1)], ring_send.at[0])
        take(nb.at[pl.ds(0, Z - 1), pl.ds(0, 256)], ring_send.at[1])
        take(nb.at[:, pl.ds(0, 256)], pair_send)
    drains.append(drain_rings)
    part_copies = []
    for k in (2, 1, 3, 0):
        target = wrap(x + k, X)
        rows = pl.ds(pl.multiple_of(target * ROWS, ROWS), ROWS)
        part[rows, :] += product(nb[last_data, rows, :], dd[c, last_data])

        @pl.when(last_data != last_noise)
        def _():
            part[rows, :] += product(nb[last_noise, rows, :], dd[c, last_noise])

        if k:
            copy = send(
                part.at[rows], part_in.at[k - 1], part_s.at[k - 1], part_r.at[k - 1],
                at(y, target, z, c),
            )
            copy.start()
            part_copies.append(copy)
    square_sum[...] += squares(dd[c, wrap(y + 4, Y)])
    norm_slots[x] = jnp.sum(jnp.transpose(square_sum[...]), axis=0, keepdims=True)
    for k in range(1, X):
        send(
            norm_slots.at[x], norm_slots.at[x], norm_s, norm_r, at(y, wrap(x + k, X), z, c)
        ).start()
    fold = squares(noise_ref[...])
    noise_squares = jnp.sum(jnp.transpose(fold), axis=0, keepdims=True)
    for copy in part_copies:
        copy.wait_recv()
    total = part[pl.ds(pl.multiple_of(x * ROWS, ROWS), ROWS), :]
    total = total + part_in[0] + part_in[1] + part_in[2]
    score[...] = total * (2.0 / LATENT / EPSILON)
    score_t[...] = jnp.transpose(score[...])
    take(norm_slots.at[pl.ds(0, X - 1)], norm_r)
    data_norm = (norm_slots[0] + norm_slots[1] + norm_slots[2] + norm_slots[3]) / LATENT

    def drain_parts():
        for copy in part_copies:
            copy.wait_send()
        take(norm_slots.at[pl.ds(0, X - 1)], norm_s)
    drains.append(drain_parts)
    dpair = send(dd.at[c], dd.at[c], dpair_send, dpair_recv, at(y, x, z, other))

    def far_first(i, n):
        return n // 2 + (1 - 2 * lax.rem(i, 2)) * ((i + 1) // 2)

    def along_col(k):
        i = (k - 1) // 2
        return at(y, x, wrap(z + far_first(i, Z), Z), wrap(c + lax.rem(k, 2), 2))

    def along_both(k):
        i, j = (k - 1) // (2 * X), lax.rem((k - 1) // 2, X)
        z_, x_ = wrap(z + far_first(i, Z), Z), wrap(x + far_first(j, X), X)
        return at(y, x_, z_, wrap(c + lax.rem(k, 2), 2))

    def along_row(k):
        i, j = (k - 1) // X, lax.rem(k - 1, X)
        return at(wrap(y + far_first(i, Y), Y), wrap(x + far_first(j, X), X), z, c)

    def post(scores, slots, step, me, count, target, send_sem, recv_sem):
        peak = jnp.max(scores, axis=0, keepdims=True)
        slots[step, me, 0:1, :] = peak
        slots[step, me, 1:2, :] = jnp.sum(jnp.exp(scores - peak), axis=0, keepdims=True)

        @pl.loop(1, count)
        def _(k):
            ref = slots.at[step, me]
            send(ref, ref, send_sem.at[step], recv_sem.at[step], target(k)).start()

        return peak

    def merge(slots, step, count, recv_sem):
        take(slots.at[step, pl.ds(0, count - 1)], recv_sem.at[step])
        return combine(slots[step])

    def drain(slots, step, count, send_sem):
        take(slots.at[step, pl.ds(0, count - 1)], send_sem.at[step])

    def combine(slots):
        peaks, sums = slots[:, 0, :], slots[:, 1, :]
        peak = jnp.max(peaks, axis=0, keepdims=True)
        total = jnp.sum(sums * jnp.exp(peaks - peak), axis=0, keepdims=True)
        return -(LOG_COUNT + peak + jnp.log(total))

    def wide(u):
        tile = flip(u, 128)
        return jnp.concatenate([tile] * (COLS // 128), axis=1)

    def post_noise(step, v):
        f_slots[step, col, 2:3, :] = noise_squares
        scores = score_t[...] + flip(v, ROWS)
        return post(scores, f_slots, step, col, N_COL, along_col, f_send, f_recv)

    def post_data(step, u):
        scores = score[...] + wide(u)
        return post(scores, g_slots, step, row, N_ROW, along_row, g_send, g_recv)

    v = -data_norm / EPSILON
    for step in range(ITERS):
        post_noise(step, v)
        flush()
        drains.append(functools.partial(drain, f_slots, step, N_COL, f_send))
        u = merge(f_slots, step, N_COL, f_recv)
        post_data(step, u)
        if step == 0:
            dpair.start()
        flush()
        drains.append(functools.partial(drain, g_slots, step, N_ROW, g_send))
        v = merge(g_slots, step, N_ROW, g_recv)
    scores = score_t[...] + flip(v, ROWS)
    peak = post(scores, h_slots, 0, x * N_COL + col, X * N_COL, along_both, h_send, h_recv)
    flush()

    def to_group(src, dst, send_sem, recv_sem):
        for k in (2, 1, 3, 0):
            for flipped in (1, 0):
                if k == 0 and flipped == 0:
                    continue
                core = wrap(c + flipped, 2)
                send(src(core), dst, send_sem, recv_sem, at(y, wrap(x + k, X), z, core)).start()

    member = c * X + x
    raw = jnp.exp(score[...] + v - wide(peak)).reshape(Z, 2, 8, COLS)
    for core in range(2):
        w_send[core] = raw[:, core].reshape(Z * 8, COLS).astype(BF16)
    to_group(lambda core: w_send.at[core], w_all.at[member], w_s, w_r)
    w_all[member] = w_send[c]
    drains.append(lambda: take(h_slots.at[0, pl.ds(0, X * N_COL - 1)], h_send.at[0]))
    take(h_slots.at[0, pl.ds(0, X * N_COL - 1)], h_recv.at[0])
    us, factors = [], [None] * (2 * X)
    for k in range(X):
        us.append(combine(h_slots[0, pl.ds(k * N_COL, N_COL)]))
        for core in range(2):
            source = h_slots[0, k * N_COL + z * 2 + core]
            factors[core * X + k] = jnp.exp(us[k] + source[0:1, :] + LOG_COUNT)
    u = us[0]
    for k in range(1, X):
        u = jnp.where(x == k, us[k], u)
    noise_norm = jnp.sum(f_slots[0, :, 2, :], axis=0, keepdims=True) / LATENT
    noise_pot_ref[...] = EPSILON * u + noise_norm
    data_pot_ref[...] = EPSILON * v + data_norm
    dpair.wait_recv()

    drains.append(dpair.wait_send)
    take(w_all.at[pl.ds(0, 2 * X - 1)], w_r)
    factors = jnp.transpose(jnp.concatenate(factors, axis=0)).reshape(Z, 2, 8, 2 * X)
    factors = jnp.where(c == 0, factors[:, 0], factors[:, 1]).reshape(Z * 8, 2 * X)
    for k in range(2 * X):
        w_all[k] = (w_all[k].astype(F32) * factors[:, k : k + 1]).astype(BF16)
    drains.append(lambda: take(w_all.at[pl.ds(0, 2 * X - 1)], w_s))
    def rs(way, piece, step):
        sign = 1 - 2 * way
        index = (way, piece, step - 1)
        if step == 1:
            src = po.at[piece, wrap(z + sign * turns(way, piece), Z)]
        else:
            src = rs_out.at[way, piece, step - 2]
        return send(
            src, rs_in.at[index], rs_s.at[index], rs_r.at[index], at(y, x, wrap(z + sign, Z), c)
        )

    for piece in range(PIECES):
        @pl.loop(0, Y // PIECES)
        def _(j):
            block = piece * (Y // PIECES) + j
            sums = jnp.dot(
                w_all[0:X].reshape(256, COLS), dd[0, block], preferred_element_type=F32
            ) + jnp.dot(w_all[X:].reshape(256, COLS), dd[1, block], preferred_element_type=F32)
            sums = sums.reshape(X, Z, 8, BLOCK)
            columns = pl.ds(pl.multiple_of(j * BLOCK, BLOCK), BLOCK)
            for k in range(Z):
                po[piece, k, :, columns] = sums[:, k].reshape(X * 8, BLOCK).astype(BF16)

        for way in range(2):
            rs(way, piece, 1).start()

    def finish(piece):
        sums = po[piece, z].astype(F32)
        for way in range(2):
            sums = sums + rs_in[way, piece, turns(way, piece) - 1].astype(F32)
        for k in range(X):
            lines = sums[k * 8 : k * 8 + 8]
            lines = jnp.concatenate([lines[:, : PIECE // 2], lines[:, PIECE // 2 :]], axis=0)
            fin_send[piece, k] = lines.astype(BF16)
        for k in (2, 1, 3):
            target = wrap(x + k, X)
            send(
                fin_send.at[piece, target], fin_in.at[piece, x], fin_s.at[piece], fin_r.at[piece],
                at(y, target, z, c),
            ).start()
        fin_in[piece, x] = fin_send[piece, x]

    flush()
    for step in range(1, 5):
        for piece in range(PIECES):
            for way in range(2):
                if step > turns(way, piece):
                    continue
                rs(way, piece, step).wait_recv()
                if step < turns(way, piece):
                    target = wrap(z + (1 - 2 * way) * (turns(way, piece) - step), Z)
                    rs_out[way, piece, step - 1] = (
                        rs_in[way, piece, step - 1].astype(F32) + po[piece, target].astype(F32)
                    ).astype(BF16)
                    rs(way, piece, step + 1).start()
            if step == 4:
                finish(piece)

    def drain_rs():
        for piece in range(PIECES):
            for way in range(2):
                for step in range(1, turns(way, piece) + 1):
                    rs(way, piece, step).wait_send()
    drain_rs()
    for piece in range(PIECES):
        take(fin_in.at[piece, pl.ds(0, X - 1)], fin_r.at[piece])
        for k in range(X):
            lines = fin_in[piece, k].astype(F32)
            for part_block in range(Y // PIECES):
                block = piece * (Y // PIECES) + part_block
                begin = (block * X + k) * BLOCK
                out_ref[:, begin : begin + BLOCK] = lines[
                    part_block * 8 : part_block * 8 + 8
                ].astype(BF16)

    def drain_fin():
        for piece in range(PIECES):
            take(fin_in.at[piece, pl.ds(0, X - 1)], fin_s.at[piece])
    drains.append(drain_fin)
    flush()


def per_device(noise, data):
    vmem = pl.BlockSpec(memory_space=pltpu.VMEM)
    dma = pltpu.SemaphoreType.DMA
    targets, noise_pot, data_pot = pl.pallas_call(
        kernel,
        out_shape=(
            jax.ShapeDtypeStruct((8, LATENT), BF16),
            jax.ShapeDtypeStruct((1, ROWS), F32),
            jax.ShapeDtypeStruct((1, COLS), F32),
        ),
        in_specs=[pl.BlockSpec(memory_space=pltpu.HBM)] * 2,
        out_specs=(vmem, vmem, vmem),
        scratch_shapes=[
            pltpu.VMEM((ROWS, 1024), BF16), dma((2,)),
            pltpu.VMEM((Z, X * ROWS, BLOCK), BF16),
            pltpu.VMEM((2, Y, COLS, BLOCK), BF16),
            pltpu.VMEM((X * ROWS, COLS), F32),
            pltpu.VMEM((X - 1, ROWS, COLS), F32),
            pltpu.VMEM((COLS, 128), F32),
            pltpu.VMEM((X, 1, COLS), F32),
            pltpu.VMEM((ROWS, COLS), F32),
            pltpu.VMEM((COLS, ROWS), F32),
            pltpu.VMEM((ITERS, N_COL, 3, ROWS), F32),
            pltpu.VMEM((ITERS, N_ROW, 2, COLS), F32),
            pltpu.VMEM((2, Z * 8, COLS), BF16),
            pltpu.VMEM((2 * X, Z * 8, COLS), BF16),
            pltpu.VMEM((1, X * N_COL, 2, ROWS), F32),
            pltpu.VMEM((PIECES, Z, X * 8, PIECE), BF16),
            pltpu.VMEM((2, PIECES, 4, X * 8, PIECE), BF16),
            pltpu.VMEM((2, PIECES, 3, X * 8, PIECE), BF16),
            pltpu.VMEM((PIECES, X, 16, PIECE // 2), BF16),
            pltpu.VMEM((PIECES, X, 16, PIECE // 2), BF16),
            dma((2, CHUNKS // 2)), dma((2, CHUNKS // 2)),
            dma((2,)), dma((2, 2, CHUNKS, 4)),
            dma, dma((2, CHUNKS, 5)), dma, dma,
            dma((3,)), dma((3,)), dma, dma,
            dma((ITERS,)), dma((ITERS,)), dma((ITERS,)), dma((ITERS,)), dma, dma, dma((1,)), dma((1,)),
            dma((2, PIECES, 4)), dma((2, PIECES, 4)), dma((PIECES,)), dma((PIECES,)),
        ],
        compiler_params=pltpu.CompilerParams(
            collective_id=0, has_side_effects=True, vmem_limit_bytes=60 * 2**20
        ),
        name="coupling",
    )(noise, data)
    return (targets, noise_pot[0], data_pot[0])


def solution(mesh):
    placed = (P("row", "col"), P("col", "row"))
    return jax.shard_map(
        per_device,
        mesh=mesh,
        in_specs=placed,
        out_specs=(P(("row", "col"), None), P("row"), P("col")),
        check_vma=False,
    )
```

```python
import functools
import math

import jax
import jax.numpy as jnp
from jax import lax
from jax.experimental import pallas as pl
from jax.experimental.pallas import tpu as pltpu
from jax.sharding import PartitionSpec as P

LATENT = 16384
ITERS = 3
X, Y, Z = 4, 8, 8
N_ROW, N_COL = X * Y, 2 * Z
ROWS, COLS = 128, 256
LOG_COUNT = math.log(4096)
EPSILON = 0.64 / math.sqrt(LATENT)
BLOCK = 512
CHUNKS = 4
CHUNK = 256 // CHUNKS
PIECES = 4
PIECE = Y * BLOCK // PIECES
MESH = pl.DeviceIdType.MESH
F32, BF16 = jnp.float32, jnp.bfloat16


def flip(line, copies):
    return jnp.transpose(jnp.broadcast_to(line, (copies, line.shape[1])))


def squares(block):
    block = jnp.square(block.astype(F32))
    return sum(block[:, i : i + 128] for i in range(0, block.shape[1], 128))


def hops(way, half):
    return 4 if way == half else 3


def legs(way, chunk):
    return hops(way, chunk // (CHUNKS // 2))


def turns(way, piece):
    return hops(way, piece // (PIECES // 2))


def kernel(
    noise_hbm, data_hbm, out_ref, noise_pot_ref, data_pot_ref,
    noise_ref, in_sem, nb, dd, part, part_in, square_sum, norm_slots, score, score_t, f_slots, g_slots,
    w_send, w_all, h_slots, po, rs_in, rs_out, fin_send, fin_in,
    own_send, own_recv, ring_send, ring_recv, pair_send, pair_recv, dpair_send, dpair_recv,
    part_s, part_r, norm_s, norm_r, f_send, f_recv, g_send, g_recv, w_s, w_r, h_send, h_recv,
    rs_s, rs_r, fin_s, fin_r,
):
    row, col = lax.axis_index("row"), lax.axis_index("col")
    y, x = row // X, lax.rem(row, X)
    z, c = col // 2, lax.rem(col, 2)
    other = 1 - c

    def at(y_, x_, z_, c_):
        return (y_ * X + x_, z_ * 2 + c_)

    def wrap(i, n):
        return lax.rem(i + n, n)

    def send(src, dst, send_sem, recv_sem, device):
        return pltpu.make_async_remote_copy(
            src_ref=src, dst_ref=dst, send_sem=send_sem, recv_sem=recv_sem,
            device_id=device, device_id_type=MESH,
        )

    def take(ref, sem):
        pltpu.make_async_copy(ref, ref, sem).wait()

    drains = []

    def flush():
        while drains:
            drains.pop(0)()

    data_ref = dd.at[c, y]
    noise_in = pltpu.make_async_copy(noise_hbm, noise_ref, in_sem.at[0])
    data_in = pltpu.make_async_copy(data_hbm, data_ref, in_sem.at[1])
    noise_in.start()
    data_in.start()

    barrier = pltpu.get_barrier_semaphore()
    near = [at(wrap(y + 1, Y), x, z, c), at(wrap(y - 1, Y), x, z, c)]
    near += [at(y, x, wrap(z + 1, Z), c), at(y, x, wrap(z - 1, Z), c), at(y, x, z, other)]
    for k in range(1, X):
        near += [at(y, wrap(x + k, X), z, c), at(y, wrap(x + k, X), z, other)]
    for device in near:
        pl.semaphore_signal(barrier, inc=1, device_id=device, device_id_type=MESH)
    part[...] = jnp.zeros_like(part)
    noise_in.wait()
    data_in.wait()
    pl.semaphore_wait(barrier, len(near))

    mine = x // 2 == c
    first = jnp.where(mine, lax.rem(x, 2), 1 - lax.rem(x, 2))

    def noise_chunk(block, core, chunk):
        half, rest = chunk // (CHUNKS // 2), chunk % (CHUNKS // 2)
        begin = core * 256 + jnp.where(first == half, 0, 1) * 128 + rest * CHUNK
        return nb.at[block, pl.ds(pl.multiple_of(begin, CHUNK), CHUNK)]

    def ring(kind, way, chunk, step):
        place = (y, z)[kind]
        sign = 1 - 2 * way
        block = wrap(place - sign * (step - 1), 8)
        target = wrap(place + sign, 8)
        if kind == 0:
            ref = dd.at[c, block, pl.ds(chunk * CHUNK, CHUNK)]
            device = at(target, x, z, c)
        else:
            ref = noise_chunk(block, c, chunk)
            device = at(y, x, target, c)
        index = (kind, way, chunk, step - 1)
        return send(ref, ref, ring_send.at[kind], ring_recv.at[index], device)

    n1_device = [at(y, 2 * c + h, z, x // 2) for h in range(2)]
    n1_self = [jnp.logical_and(mine, lax.rem(x, 2) == h) for h in range(2)]
    n1 = []
    for rest in range(CHUNKS // 2):
        for h in range(2):
            src = noise_ref.at[pl.ds(rest * CHUNK, CHUNK), pl.ds(h * BLOCK, BLOCK)]
            dst = nb.at[z, pl.ds(pl.multiple_of(x * ROWS + rest * CHUNK, CHUNK), CHUNK)]
            sem = own_recv.at[lax.rem(x, 2), rest]
            far = send(src, dst, own_send.at[h, rest], sem, n1_device[h])
            near_copy = pltpu.make_async_copy(src, dst, sem)
            n1.append((h, far))

            @pl.when(n1_self[h])
            def _():
                near_copy.start()

            @pl.when(jnp.logical_not(n1_self[h]))
            def _():
                far.start()

    for chunk in range(CHUNKS):
        for way in range(2):
            ring(0, way, chunk, 1).start()

    def pair(way, chunk, step, block):
        index = (way, chunk, step)
        ref = noise_chunk(block, c, chunk)
        return send(ref, ref, pair_send, pair_recv.at[index], at(y, x, z, other))

    pairs = []
    for chunk in range(CHUNKS):
        half, rest = chunk // (CHUNKS // 2), chunk % (CHUNKS // 2)
        parity = jnp.where(first == half, 0, 1)
        take(noise_chunk(z, c, chunk), own_recv.at[parity, rest])
        for way in range(2):
            ring(1, way, chunk, 1).start()
        pairs.append(pair(0, chunk, 0, z))
        pairs[-1].start()

    square_sum[...] = squares(data_ref[...])
    last_data, last_noise = wrap(y + 4, Y), wrap(z + 4, Z)

    def product(a, b):
        return lax.dot_general(a, b, (((1,), (1,)), ((), ())), preferred_element_type=F32)

    for step in range(1, 5):
        for chunk in range(CHUNKS):
            for kind in range(2):
                for way in range(2):
                    if step > legs(way, chunk):
                        continue
                    ring(kind, way, chunk, step).wait_recv()
                    if step < legs(way, chunk):
                        ring(kind, way, chunk, step + 1).start()
                    if kind == 1:
                        block = wrap(z - (1 - 2 * way) * step, Z)
                        pairs.append(pair(way, chunk, step, block))
                        pairs[-1].start()
        if step < 4:
            for block in (wrap(y - step, Y), wrap(y + step, Y)):
                square_sum[...] += squares(dd[c, block])
        if step == 3:
            for copy in pairs:
                copy.wait_recv()
            early = len(pairs)

            @pl.loop(0, Y)
            def _(k):
                @pl.when(jnp.logical_and(k != last_data, k != last_noise))
                def _():
                    part[...] += product(nb[k], dd[c, k])
    for copy in pairs[early:]:
        copy.wait_recv()

    def drain_rings():
        for h, far in n1:
            @pl.when(jnp.logical_not(n1_self[h]))
            def _():
                far.wait_send()
        take(dd.at[c, pl.ds(0, Y - 1)], ring_send.at[0])
        take(nb.at[pl.ds(0, Z - 1), pl.ds(0, 256)], ring_send.at[1])
        take(nb.at[:, pl.ds(0, 256)], pair_send)
    drains.append(drain_rings)
    part_copies = []
    for k in (2, 1, 3, 0):
        target = wrap(x + k, X)
        rows = pl.ds(pl.multiple_of(target * ROWS, ROWS), ROWS)
        part[rows, :] += product(nb[last_data, rows, :], dd[c, last_data])

        @pl.when(last_data != last_noise)
        def _():
            part[rows, :] += product(nb[last_noise, rows, :], dd[c, last_noise])

        if k:
            copy = send(
                part.at[rows], part_in.at[k - 1], part_s.at[k - 1], part_r.at[k - 1],
                at(y, target, z, c),
            )
            copy.start()
            part_copies.append(copy)
    square_sum[...] += squares(dd[c, wrap(y + 4, Y)])
    norm_slots[x] = jnp.sum(jnp.transpose(square_sum[...]), axis=0, keepdims=True)
    for k in range(1, X):
        send(
            norm_slots.at[x], norm_slots.at[x], norm_s, norm_r, at(y, wrap(x + k, X), z, c)
        ).start()
    fold = squares(noise_ref[...])
    noise_squares = jnp.sum(jnp.transpose(fold), axis=0, keepdims=True)
    for copy in part_copies:
        copy.wait_recv()
    total = part[pl.ds(pl.multiple_of(x * ROWS, ROWS), ROWS), :]
    total = total + part_in[0] + part_in[1] + part_in[2]
    score[...] = total * (2.0 / LATENT / EPSILON)
    score_t[...] = jnp.transpose(score[...])
    take(norm_slots.at[pl.ds(0, X - 1)], norm_r)
    data_norm = (norm_slots[0] + norm_slots[1] + norm_slots[2] + norm_slots[3]) / LATENT

    def drain_parts():
        for copy in part_copies:
            copy.wait_send()
        take(norm_slots.at[pl.ds(0, X - 1)], norm_s)
    drains.append(drain_parts)
    dpair = send(dd.at[c], dd.at[c], dpair_send, dpair_recv, at(y, x, z, other))

    def far_first(i, n):
        return n // 2 + (1 - 2 * lax.rem(i, 2)) * ((i + 1) // 2)

    def along_col(k):
        i = (k - 1) // 2
        return at(y, x, wrap(z + far_first(i, Z), Z), wrap(c + lax.rem(k, 2), 2))

    def along_both(k):
        i, j = (k - 1) // (2 * X), lax.rem((k - 1) // 2, X)
        z_, x_ = wrap(z + far_first(i, Z), Z), wrap(x + far_first(j, X), X)
        return at(y, x_, z_, wrap(c + lax.rem(k, 2), 2))

    def along_row(k):
        i, j = (k - 1) // X, lax.rem(k - 1, X)
        return at(wrap(y + far_first(i, Y), Y), wrap(x + far_first(j, X), X), z, c)

    def post(scores, slots, step, me, count, target, send_sem, recv_sem):
        peak = jnp.max(scores, axis=0, keepdims=True)
        slots[step, me, 0:1, :] = peak
        slots[step, me, 1:2, :] = jnp.sum(jnp.exp(scores - peak), axis=0, keepdims=True)

        @pl.loop(1, count)
        def _(k):
            ref = slots.at[step, me]
            send(ref, ref, send_sem.at[step], recv_sem.at[step], target(k)).start()

        return peak

    def merge(slots, step, count, recv_sem):
        take(slots.at[step, pl.ds(0, count - 1)], recv_sem.at[step])
        return combine(slots[step])

    def drain(slots, step, count, send_sem):
        take(slots.at[step, pl.ds(0, count - 1)], send_sem.at[step])

    def combine(slots):
        peaks, sums = slots[:, 0, :], slots[:, 1, :]
        peak = jnp.max(peaks, axis=0, keepdims=True)
        total = jnp.sum(sums * jnp.exp(peaks - peak), axis=0, keepdims=True)
        return -(LOG_COUNT + peak + jnp.log(total))

    def wide(u):
        tile = flip(u, 128)
        return jnp.concatenate([tile] * (COLS // 128), axis=1)

    def post_noise(step, v):
        f_slots[step, col, 2:3, :] = noise_squares
        scores = score_t[...] + flip(v, ROWS)
        return post(scores, f_slots, step, col, N_COL, along_col, f_send, f_recv)

    def post_data(step, u):
        scores = score[...] + wide(u)
        return post(scores, g_slots, step, row, N_ROW, along_row, g_send, g_recv)

    v = -data_norm / EPSILON
    for step in range(ITERS):
        post_noise(step, v)
        flush()
        drains.append(functools.partial(drain, f_slots, step, N_COL, f_send))
        u = merge(f_slots, step, N_COL, f_recv)
        post_data(step, u)
        if step == 0:
            dpair.start()
        flush()
        drains.append(functools.partial(drain, g_slots, step, N_ROW, g_send))
        v = merge(g_slots, step, N_ROW, g_recv)
    scores = score_t[...] + flip(v, ROWS)
    peak = post(scores, h_slots, 0, x * N_COL + col, X * N_COL, along_both, h_send, h_recv)
    flush()

    def to_group(src, dst, send_sem, recv_sem):
        for k in (2, 1, 3, 0):
            for flipped in (1, 0):
                if k == 0 and flipped == 0:
                    continue
                core = wrap(c + flipped, 2)
                send(src(core), dst, send_sem, recv_sem, at(y, wrap(x + k, X), z, core)).start()

    member = c * X + x
    raw = jnp.exp(score[...] + v - wide(peak)).reshape(Z, 2, 8, COLS)
    for core in range(2):
        w_send[core] = raw[:, core].reshape(Z * 8, COLS).astype(BF16)
    to_group(lambda core: w_send.at[core], w_all.at[member], w_s, w_r)
    w_all[member] = w_send[c]
    drains.append(lambda: take(h_slots.at[0, pl.ds(0, X * N_COL - 1)], h_send.at[0]))
    take(h_slots.at[0, pl.ds(0, X * N_COL - 1)], h_recv.at[0])
    us, factors = [], [None] * (2 * X)
    for k in range(X):
        us.append(combine(h_slots[0, pl.ds(k * N_COL, N_COL)]))
        for core in range(2):
            source = h_slots[0, k * N_COL + z * 2 + core]
            factors[core * X + k] = jnp.exp(us[k] + source[0:1, :] + LOG_COUNT)
    u = us[0]
    for k in range(1, X):
        u = jnp.where(x == k, us[k], u)
    noise_norm = jnp.sum(f_slots[0, :, 2, :], axis=0, keepdims=True) / LATENT
    noise_pot_ref[...] = EPSILON * u + noise_norm
    data_pot_ref[...] = EPSILON * v + data_norm
    dpair.wait_recv()

    drains.append(dpair.wait_send)
    take(w_all.at[pl.ds(0, 2 * X - 1)], w_r)
    factors = jnp.transpose(jnp.concatenate(factors, axis=0)).reshape(Z, 2, 8, 2 * X)
    factors = jnp.where(c == 0, factors[:, 0], factors[:, 1]).reshape(Z * 8, 2 * X)
    for k in range(2 * X):
        w_all[k] = (w_all[k].astype(F32) * factors[:, k : k + 1]).astype(BF16)
    drains.append(lambda: take(w_all.at[pl.ds(0, 2 * X - 1)], w_s))
    def rs(way, piece, step):
        sign = 1 - 2 * way
        index = (way, piece, step - 1)
        if step == 1:
            src = po.at[piece, wrap(z + sign * turns(way, piece), Z)]
        else:
            src = rs_out.at[way, piece, step - 2]
        return send(
            src, rs_in.at[index], rs_s.at[index], rs_r.at[index], at(y, x, wrap(z + sign, Z), c)
        )

    for piece in range(PIECES):
        @pl.loop(0, Y // PIECES)
        def _(j):
            block = piece * (Y // PIECES) + j
            sums = jnp.dot(
                w_all[0:X].reshape(256, COLS), dd[0, block], preferred_element_type=F32
            ) + jnp.dot(w_all[X:].reshape(256, COLS), dd[1, block], preferred_element_type=F32)
            sums = sums.reshape(X, Z, 8, BLOCK)
            columns = pl.ds(pl.multiple_of(j * BLOCK, BLOCK), BLOCK)
            for k in range(Z):
                po[piece, k, :, columns] = sums[:, k].reshape(X * 8, BLOCK).astype(BF16)

        for way in range(2):
            rs(way, piece, 1).start()

    def finish(piece):
        sums = po[piece, z].astype(F32)
        for way in range(2):
            sums = sums + rs_in[way, piece, turns(way, piece) - 1].astype(F32)
        for k in range(X):
            lines = sums[k * 8 : k * 8 + 8]
            lines = jnp.concatenate([lines[:, : PIECE // 2], lines[:, PIECE // 2 :]], axis=0)
            fin_send[piece, k] = lines.astype(BF16)
        for k in (2, 1, 3):
            target = wrap(x + k, X)
            send(
                fin_send.at[piece, target], fin_in.at[piece, x], fin_s.at[piece], fin_r.at[piece],
                at(y, target, z, c),
            ).start()
        fin_in[piece, x] = fin_send[piece, x]

    flush()
    for step in range(1, 5):
        for piece in range(PIECES):
            for way in range(2):
                if step > turns(way, piece):
                    continue
                rs(way, piece, step).wait_recv()
                if step < turns(way, piece):
                    target = wrap(z + (1 - 2 * way) * (turns(way, piece) - step), Z)
                    rs_out[way, piece, step - 1] = (
                        rs_in[way, piece, step - 1].astype(F32) + po[piece, target].astype(F32)
                    ).astype(BF16)
                    rs(way, piece, step + 1).start()
            if step == 4:
                finish(piece)

    def drain_rs():
        for piece in range(PIECES):
            for way in range(2):
                for step in range(1, turns(way, piece) + 1):
                    rs(way, piece, step).wait_send()
    drain_rs()
    for piece in range(PIECES):
        take(fin_in.at[piece, pl.ds(0, X - 1)], fin_r.at[piece])
        for k in range(X):
            lines = fin_in[piece, k].astype(F32)
            for part_piece in range(2):
                block, inner = divmod(piece * PIECE + part_piece * (PIECE // 2), BLOCK)
                begin = (block * X + k) * BLOCK + inner
                out_ref[:, begin : begin + PIECE // 2] = lines[
                    part_piece * 8 : part_piece * 8 + 8
                ].astype(BF16)

    def drain_fin():
        for piece in range(PIECES):
            take(fin_in.at[piece, pl.ds(0, X - 1)], fin_s.at[piece])
    drains.append(drain_fin)
    flush()


def per_device(noise, data):
    vmem = pl.BlockSpec(memory_space=pltpu.VMEM)
    dma = pltpu.SemaphoreType.DMA
    targets, noise_pot, data_pot = pl.pallas_call(
        kernel,
        out_shape=(
            jax.ShapeDtypeStruct((8, LATENT), BF16),
            jax.ShapeDtypeStruct((1, ROWS), F32),
            jax.ShapeDtypeStruct((1, COLS), F32),
        ),
        in_specs=[pl.BlockSpec(memory_space=pltpu.HBM)] * 2,
        out_specs=(vmem, vmem, vmem),
        scratch_shapes=[
            pltpu.VMEM((ROWS, 1024), BF16), dma((2,)),
            pltpu.VMEM((Z, X * ROWS, BLOCK), BF16),
            pltpu.VMEM((2, Y, COLS, BLOCK), BF16),
            pltpu.VMEM((X * ROWS, COLS), F32),
            pltpu.VMEM((X - 1, ROWS, COLS), F32),
            pltpu.VMEM((COLS, 128), F32),
            pltpu.VMEM((X, 1, COLS), F32),
            pltpu.VMEM((ROWS, COLS), F32),
            pltpu.VMEM((COLS, ROWS), F32),
            pltpu.VMEM((ITERS, N_COL, 3, ROWS), F32),
            pltpu.VMEM((ITERS, N_ROW, 2, COLS), F32),
            pltpu.VMEM((2, Z * 8, COLS), BF16),
            pltpu.VMEM((2 * X, Z * 8, COLS), BF16),
            pltpu.VMEM((1, X * N_COL, 2, ROWS), F32),
            pltpu.VMEM((PIECES, Z, X * 8, PIECE), BF16),
            pltpu.VMEM((2, PIECES, 4, X * 8, PIECE), BF16),
            pltpu.VMEM((2, PIECES, 3, X * 8, PIECE), BF16),
            pltpu.VMEM((PIECES, X, 16, PIECE // 2), BF16),
            pltpu.VMEM((PIECES, X, 16, PIECE // 2), BF16),
            dma((2, CHUNKS // 2)), dma((2, CHUNKS // 2)),
            dma((2,)), dma((2, 2, CHUNKS, 4)),
            dma, dma((2, CHUNKS, 5)), dma, dma,
            dma((3,)), dma((3,)), dma, dma,
            dma((ITERS,)), dma((ITERS,)), dma((ITERS,)), dma((ITERS,)), dma, dma, dma((1,)), dma((1,)),
            dma((2, PIECES, 4)), dma((2, PIECES, 4)), dma((PIECES,)), dma((PIECES,)),
        ],
        compiler_params=pltpu.CompilerParams(
            collective_id=0, has_side_effects=True, vmem_limit_bytes=107 * 2**19
        ),
        name="coupling",
    )(noise, data)
    return (targets, noise_pot[0], data_pot[0])


def solution(mesh):
    placed = (P("row", "col"), P("col", "row"))
    return jax.shard_map(
        per_device,
        mesh=mesh,
        in_specs=placed,
        out_specs=(P(("row", "col"), None), P("row"), P("col")),
        check_vma=False,
    )
```

```python
import functools
import math

import jax
import jax.numpy as jnp
from jax import lax
from jax.experimental import pallas as pl
from jax.experimental.pallas import tpu as pltpu
from jax.sharding import PartitionSpec as P

LATENT = 16384
ITERS = 3
X, Y, Z = 4, 8, 8
N_ROW, N_COL = X * Y, 2 * Z
ROWS, COLS = 128, 256
LOG_COUNT = math.log(4096)
EPSILON = 0.64 / math.sqrt(LATENT)
BLOCK = 512
CHUNKS = 4
CHUNK = 256 // CHUNKS
PIECES = 4
PIECE = Y * BLOCK // PIECES
MESH = pl.DeviceIdType.MESH
F32, BF16 = jnp.float32, jnp.bfloat16


def flip(line, copies):
    return jnp.transpose(jnp.broadcast_to(line, (copies, line.shape[1])))


def squares(block):
    block = jnp.square(block.astype(F32))
    return sum(block[:, i : i + 128] for i in range(0, block.shape[1], 128))


def hops(way, half):
    return 4 if way == half else 3


def legs(way, chunk):
    return hops(way, chunk // (CHUNKS // 2))


def turns(way, piece):
    return hops(way, piece // (PIECES // 2))


def kernel(
    noise_hbm, data_hbm, out_ref, noise_pot_ref, data_pot_ref,
    noise_ref, in_sem, nb, dd, part, part_in, square_sum, norm_slots, score, score_t, f_slots, g_slots,
    w_send, w_all, h_slots, po, rs_in, rs_out, fin_send, fin_in,
    own_send, own_recv, ring_send, ring_recv, pair_send, pair_recv, dpair_send, dpair_recv,
    part_s, part_r, norm_s, norm_r, f_send, f_recv, g_send, g_recv, w_s, w_r, h_send, h_recv,
    rs_s, rs_r, fin_s, fin_r,
):
    row, col = lax.axis_index("row"), lax.axis_index("col")
    y, x = row // X, lax.rem(row, X)
    z, c = col // 2, lax.rem(col, 2)
    other = 1 - c

    def at(y_, x_, z_, c_):
        return (y_ * X + x_, z_ * 2 + c_)

    def wrap(i, n):
        return lax.rem(i + n, n)

    def send(src, dst, send_sem, recv_sem, device):
        return pltpu.make_async_remote_copy(
            src_ref=src, dst_ref=dst, send_sem=send_sem, recv_sem=recv_sem,
            device_id=device, device_id_type=MESH,
        )

    def take(ref, sem):
        pltpu.make_async_copy(ref, ref, sem).wait()

    drains = []

    def flush():
        while drains:
            drains.pop(0)()

    data_ref = dd.at[c, y]
    noise_in = pltpu.make_async_copy(noise_hbm, noise_ref, in_sem.at[0])
    data_in = pltpu.make_async_copy(data_hbm, data_ref, in_sem.at[1])
    noise_in.start()
    data_in.start()

    barrier = pltpu.get_barrier_semaphore()
    near = [at(wrap(y + 1, Y), x, z, c), at(wrap(y - 1, Y), x, z, c)]
    near += [at(y, x, wrap(z + 1, Z), c), at(y, x, wrap(z - 1, Z), c), at(y, x, z, other)]
    for k in range(1, X):
        near += [at(y, wrap(x + k, X), z, c), at(y, wrap(x + k, X), z, other)]
    for device in near:
        pl.semaphore_signal(barrier, inc=1, device_id=device, device_id_type=MESH)
    part[...] = jnp.zeros_like(part)
    noise_in.wait()
    data_in.wait()
    pl.semaphore_wait(barrier, len(near))

    mine = x // 2 == c
    first = jnp.where(mine, lax.rem(x, 2), 1 - lax.rem(x, 2))

    def noise_chunk(block, core, chunk):
        half, rest = chunk // (CHUNKS // 2), chunk % (CHUNKS // 2)
        begin = core * 256 + jnp.where(first == half, 0, 1) * 128 + rest * CHUNK
        return nb.at[block, pl.ds(pl.multiple_of(begin, CHUNK), CHUNK)]

    def ring(kind, way, chunk, step):
        place = (y, z)[kind]
        sign = 1 - 2 * way
        block = wrap(place - sign * (step - 1), 8)
        target = wrap(place + sign, 8)
        if kind == 0:
            ref = dd.at[c, block, pl.ds(chunk * CHUNK, CHUNK)]
            device = at(target, x, z, c)
        else:
            ref = noise_chunk(block, c, chunk)
            device = at(y, x, target, c)
        index = (kind, way, chunk, step - 1)
        return send(ref, ref, ring_send.at[kind], ring_recv.at[index], device)

    n1_device = [at(y, 2 * c + h, z, x // 2) for h in range(2)]
    n1_self = [jnp.logical_and(mine, lax.rem(x, 2) == h) for h in range(2)]
    n1 = []
    for rest in range(CHUNKS // 2):
        for h in range(2):
            src = noise_ref.at[pl.ds(rest * CHUNK, CHUNK), pl.ds(h * BLOCK, BLOCK)]
            dst = nb.at[z, pl.ds(pl.multiple_of(x * ROWS + rest * CHUNK, CHUNK), CHUNK)]
            sem = own_recv.at[lax.rem(x, 2), rest]
            far = send(src, dst, own_send.at[h, rest], sem, n1_device[h])
            near_copy = pltpu.make_async_copy(src, dst, sem)
            n1.append((h, far))

            @pl.when(n1_self[h])
            def _():
                near_copy.start()

            @pl.when(jnp.logical_not(n1_self[h]))
            def _():
                far.start()

    for chunk in range(CHUNKS):
        for way in range(2):
            ring(0, way, chunk, 1).start()

    def pair(way, chunk, step, block):
        index = (way, chunk, step)
        ref = noise_chunk(block, c, chunk)
        return send(ref, ref, pair_send, pair_recv.at[index], at(y, x, z, other))

    pairs = []
    for chunk in range(CHUNKS):
        half, rest = chunk // (CHUNKS // 2), chunk % (CHUNKS // 2)
        parity = jnp.where(first == half, 0, 1)
        take(noise_chunk(z, c, chunk), own_recv.at[parity, rest])
        for way in range(2):
            ring(1, way, chunk, 1).start()
        pairs.append(pair(0, chunk, 0, z))
        pairs[-1].start()

    square_sum[...] = squares(data_ref[...])
    last_data, last_noise = wrap(y + 4, Y), wrap(z + 4, Z)

    def product(a, b):
        return lax.dot_general(a, b, (((1,), (1,)), ((), ())), preferred_element_type=F32)

    for step in range(1, 5):
        for chunk in range(CHUNKS):
            for kind in range(2):
                for way in range(2):
                    if step > legs(way, chunk):
                        continue
                    ring(kind, way, chunk, step).wait_recv()
                    if step < legs(way, chunk):
                        ring(kind, way, chunk, step + 1).start()
                    if kind == 1:
                        block = wrap(z - (1 - 2 * way) * step, Z)
                        pairs.append(pair(way, chunk, step, block))
                        pairs[-1].start()
        if step < 4:
            for block in (wrap(y - step, Y), wrap(y + step, Y)):
                square_sum[...] += squares(dd[c, block])
        if step == 3:
            for copy in pairs:
                copy.wait_recv()
            early = len(pairs)

            @pl.loop(0, Y)
            def _(k):
                @pl.when(jnp.logical_and(k != last_data, k != last_noise))
                def _():
                    part[...] += product(nb[k], dd[c, k])
    for copy in pairs[early:]:
        copy.wait_recv()

    def drain_rings():
        for h, far in n1:
            @pl.when(jnp.logical_not(n1_self[h]))
            def _():
                far.wait_send()
        take(dd.at[c, pl.ds(0, Y - 1)], ring_send.at[0])
        take(nb.at[pl.ds(0, Z - 1), pl.ds(0, 256)], ring_send.at[1])
        take(nb.at[:, pl.ds(0, 256)], pair_send)
    drains.append(drain_rings)
    part_copies = []
    for k in (2, 1, 3, 0):
        target = wrap(x + k, X)
        rows = pl.ds(pl.multiple_of(target * ROWS, ROWS), ROWS)
        part[rows, :] += product(nb[last_data, rows, :], dd[c, last_data])

        @pl.when(last_data != last_noise)
        def _():
            part[rows, :] += product(nb[last_noise, rows, :], dd[c, last_noise])

        if k:
            copy = send(
                part.at[rows], part_in.at[k - 1], part_s.at[k - 1], part_r.at[k - 1],
                at(y, target, z, c),
            )
            copy.start()
            part_copies.append(copy)
    square_sum[...] += squares(dd[c, wrap(y + 4, Y)])
    norm_slots[x] = jnp.sum(jnp.transpose(square_sum[...]), axis=0, keepdims=True)
    for k in range(1, X):
        send(
            norm_slots.at[x], norm_slots.at[x], norm_s, norm_r, at(y, wrap(x + k, X), z, c)
        ).start()
    fold = squares(noise_ref[...])
    noise_squares = jnp.sum(jnp.transpose(fold), axis=0, keepdims=True)
    for copy in part_copies:
        copy.wait_recv()
    total = part[pl.ds(pl.multiple_of(x * ROWS, ROWS), ROWS), :]
    total = total + part_in[0] + part_in[1] + part_in[2]
    total = total * (2.0 / LATENT / EPSILON)
    score_t[...] = jnp.transpose(total)
    score[...] = total
    take(norm_slots.at[pl.ds(0, X - 1)], norm_r)
    data_norm = (norm_slots[0] + norm_slots[1] + norm_slots[2] + norm_slots[3]) / LATENT

    def drain_parts():
        for copy in part_copies:
            copy.wait_send()
        take(norm_slots.at[pl.ds(0, X - 1)], norm_s)
    drains.append(drain_parts)
    dpair = send(dd.at[c], dd.at[c], dpair_send, dpair_recv, at(y, x, z, other))

    def far_first(i, n):
        return n // 2 + (1 - 2 * lax.rem(i, 2)) * ((i + 1) // 2)

    def along_col(k):
        i = (k - 1) // 2
        return at(y, x, wrap(z + far_first(i, Z), Z), wrap(c + lax.rem(k, 2), 2))

    def along_both(k):
        i, j = (k - 1) // (2 * X), lax.rem((k - 1) // 2, X)
        z_, x_ = wrap(z + far_first(i, Z), Z), wrap(x + far_first(j, X), X)
        return at(y, x_, z_, wrap(c + lax.rem(k, 2), 2))

    def along_row(k):
        i, j = (k - 1) // X, lax.rem(k - 1, X)
        return at(wrap(y + far_first(i, Y), Y), wrap(x + far_first(j, X), X), z, c)

    def post(scores, slots, step, me, count, target, send_sem, recv_sem):
        peak = jnp.max(scores, axis=0, keepdims=True)
        slots[step, me, 0:1, :] = peak
        slots[step, me, 1:2, :] = jnp.sum(jnp.exp(scores - peak), axis=0, keepdims=True)

        @pl.loop(1, count)
        def _(k):
            ref = slots.at[step, me]
            send(ref, ref, send_sem.at[step], recv_sem.at[step], target(k)).start()

        return peak

    def merge(slots, step, count, recv_sem):
        take(slots.at[step, pl.ds(0, count - 1)], recv_sem.at[step])
        return combine(slots[step])

    def drain(slots, step, count, send_sem):
        take(slots.at[step, pl.ds(0, count - 1)], send_sem.at[step])

    def combine(slots):
        peaks, sums = slots[:, 0, :], slots[:, 1, :]
        peak = jnp.max(peaks, axis=0, keepdims=True)
        total = jnp.sum(sums * jnp.exp(peaks - peak), axis=0, keepdims=True)
        return -(LOG_COUNT + peak + jnp.log(total))

    def wide(u):
        tile = flip(u, 128)
        return jnp.concatenate([tile] * (COLS // 128), axis=1)

    def post_noise(step, v):
        f_slots[step, col, 2:3, :] = noise_squares
        scores = score_t[...] + flip(v, ROWS)
        return post(scores, f_slots, step, col, N_COL, along_col, f_send, f_recv)

    def post_data(step, u):
        scores = score[...] + wide(u)
        return post(scores, g_slots, step, row, N_ROW, along_row, g_send, g_recv)

    v = -data_norm / EPSILON
    for step in range(ITERS):
        post_noise(step, v)
        flush()
        drains.append(functools.partial(drain, f_slots, step, N_COL, f_send))
        u = merge(f_slots, step, N_COL, f_recv)
        post_data(step, u)
        if step == 0:
            dpair.start()
        flush()
        drains.append(functools.partial(drain, g_slots, step, N_ROW, g_send))
        v = merge(g_slots, step, N_ROW, g_recv)
    scores = score_t[...] + flip(v, ROWS)
    peak = post(scores, h_slots, 0, x * N_COL + col, X * N_COL, along_both, h_send, h_recv)
    flush()

    def to_group(src, dst, send_sem, recv_sem):
        for k in (2, 1, 3, 0):
            for flipped in (1, 0):
                if k == 0 and flipped == 0:
                    continue
                core = wrap(c + flipped, 2)
                send(src(core), dst, send_sem, recv_sem, at(y, wrap(x + k, X), z, core)).start()

    member = c * X + x
    raw = jnp.exp(score[...] + v - wide(peak)).reshape(Z, 2, 8, COLS)
    for core in range(2):
        w_send[core] = raw[:, core].reshape(Z * 8, COLS).astype(BF16)
    to_group(lambda core: w_send.at[core], w_all.at[member], w_s, w_r)
    w_all[member] = w_send[c]
    drains.append(lambda: take(h_slots.at[0, pl.ds(0, X * N_COL - 1)], h_send.at[0]))
    take(h_slots.at[0, pl.ds(0, X * N_COL - 1)], h_recv.at[0])
    us, factors = [], [None] * (2 * X)
    for k in range(X):
        us.append(combine(h_slots[0, pl.ds(k * N_COL, N_COL)]))
        for core in range(2):
            source = h_slots[0, k * N_COL + z * 2 + core]
            factors[core * X + k] = jnp.exp(us[k] + source[0:1, :] + LOG_COUNT)
    u = us[0]
    for k in range(1, X):
        u = jnp.where(x == k, us[k], u)
    noise_norm = jnp.sum(f_slots[0, :, 2, :], axis=0, keepdims=True) / LATENT
    noise_pot_ref[...] = EPSILON * u + noise_norm
    data_pot_ref[...] = EPSILON * v + data_norm
    dpair.wait_recv()

    drains.append(dpair.wait_send)
    take(w_all.at[pl.ds(0, 2 * X - 1)], w_r)
    factors = jnp.transpose(jnp.concatenate(factors, axis=0)).reshape(Z, 2, 8, 2 * X)
    factors = jnp.where(c == 0, factors[:, 0], factors[:, 1]).reshape(Z * 8, 2 * X)
    for k in range(2 * X):
        w_all[k] = (w_all[k].astype(F32) * factors[:, k : k + 1]).astype(BF16)
    drains.append(lambda: take(w_all.at[pl.ds(0, 2 * X - 1)], w_s))
    def rs(way, piece, step):
        sign = 1 - 2 * way
        index = (way, piece, step - 1)
        if step == 1:
            src = po.at[piece, wrap(z + sign * turns(way, piece), Z)]
        else:
            src = rs_out.at[way, piece, step - 2]
        return send(
            src, rs_in.at[index], rs_s.at[index], rs_r.at[index], at(y, x, wrap(z + sign, Z), c)
        )

    for piece in range(PIECES):
        @pl.loop(0, Y // PIECES)
        def _(j):
            block = piece * (Y // PIECES) + j
            sums = jnp.dot(
                w_all[0:X].reshape(256, COLS), dd[0, block], preferred_element_type=F32
            ) + jnp.dot(w_all[X:].reshape(256, COLS), dd[1, block], preferred_element_type=F32)
            sums = sums.reshape(X, Z, 8, BLOCK)
            columns = pl.ds(pl.multiple_of(j * BLOCK, BLOCK), BLOCK)
            for k in range(Z):
                po[piece, k, :, columns] = sums[:, k].reshape(X * 8, BLOCK).astype(BF16)

        for way in range(2):
            rs(way, piece, 1).start()

    def finish(piece):
        sums = po[piece, z].astype(F32)
        for way in range(2):
            sums = sums + rs_in[way, piece, turns(way, piece) - 1].astype(F32)
        for k in range(X):
            lines = sums[k * 8 : k * 8 + 8]
            lines = jnp.concatenate([lines[:, : PIECE // 2], lines[:, PIECE // 2 :]], axis=0)
            fin_send[piece, k] = lines.astype(BF16)
        for k in (2, 1, 3):
            target = wrap(x + k, X)
            send(
                fin_send.at[piece, target], fin_in.at[piece, x], fin_s.at[piece], fin_r.at[piece],
                at(y, target, z, c),
            ).start()
        fin_in[piece, x] = fin_send[piece, x]

    flush()
    for step in range(1, 5):
        for piece in range(PIECES):
            for way in range(2):
                if step > turns(way, piece):
                    continue
                rs(way, piece, step).wait_recv()
                if step < turns(way, piece):
                    target = wrap(z + (1 - 2 * way) * (turns(way, piece) - step), Z)
                    rs_out[way, piece, step - 1] = (
                        rs_in[way, piece, step - 1].astype(F32) + po[piece, target].astype(F32)
                    ).astype(BF16)
                    rs(way, piece, step + 1).start()
            if step == 4:
                finish(piece)

    def drain_rs():
        for piece in range(PIECES):
            for way in range(2):
                for step in range(1, turns(way, piece) + 1):
                    rs(way, piece, step).wait_send()
    drain_rs()
    for piece in range(PIECES):
        take(fin_in.at[piece, pl.ds(0, X - 1)], fin_r.at[piece])
        for k in range(X):
            lines = fin_in[piece, k].astype(F32)
            for part_piece in range(2):
                block, inner = divmod(piece * PIECE + part_piece * (PIECE // 2), BLOCK)
                begin = (block * X + k) * BLOCK + inner
                out_ref[:, begin : begin + PIECE // 2] = lines[
                    part_piece * 8 : part_piece * 8 + 8
                ].astype(BF16)

    def drain_fin():
        for piece in range(PIECES):
            take(fin_in.at[piece, pl.ds(0, X - 1)], fin_s.at[piece])
    drains.append(drain_fin)
    flush()


def per_device(noise, data):
    vmem = pl.BlockSpec(memory_space=pltpu.VMEM)
    dma = pltpu.SemaphoreType.DMA
    targets, noise_pot, data_pot = pl.pallas_call(
        kernel,
        out_shape=(
            jax.ShapeDtypeStruct((8, LATENT), BF16),
            jax.ShapeDtypeStruct((1, ROWS), F32),
            jax.ShapeDtypeStruct((1, COLS), F32),
        ),
        in_specs=[pl.BlockSpec(memory_space=pltpu.HBM)] * 2,
        out_specs=(vmem, vmem, vmem),
        scratch_shapes=[
            pltpu.VMEM((ROWS, 1024), BF16), dma((2,)),
            pltpu.VMEM((Z, X * ROWS, BLOCK), BF16),
            pltpu.VMEM((2, Y, COLS, BLOCK), BF16),
            pltpu.VMEM((X * ROWS, COLS), F32),
            pltpu.VMEM((X - 1, ROWS, COLS), F32),
            pltpu.VMEM((COLS, 128), F32),
            pltpu.VMEM((X, 1, COLS), F32),
            pltpu.VMEM((ROWS, COLS), F32),
            pltpu.VMEM((COLS, ROWS), F32),
            pltpu.VMEM((ITERS, N_COL, 3, ROWS), F32),
            pltpu.VMEM((ITERS, N_ROW, 2, COLS), F32),
            pltpu.VMEM((2, Z * 8, COLS), BF16),
            pltpu.VMEM((2 * X, Z * 8, COLS), BF16),
            pltpu.VMEM((1, X * N_COL, 2, ROWS), F32),
            pltpu.VMEM((PIECES, Z, X * 8, PIECE), BF16),
            pltpu.VMEM((2, PIECES, 4, X * 8, PIECE), BF16),
            pltpu.VMEM((2, PIECES, 3, X * 8, PIECE), BF16),
            pltpu.VMEM((PIECES, X, 16, PIECE // 2), BF16),
            pltpu.VMEM((PIECES, X, 16, PIECE // 2), BF16),
            dma((2, CHUNKS // 2)), dma((2, CHUNKS // 2)),
            dma((2,)), dma((2, 2, CHUNKS, 4)),
            dma, dma((2, CHUNKS, 5)), dma, dma,
            dma((3,)), dma((3,)), dma, dma,
            dma((ITERS,)), dma((ITERS,)), dma((ITERS,)), dma((ITERS,)), dma, dma, dma((1,)), dma((1,)),
            dma((2, PIECES, 4)), dma((2, PIECES, 4)), dma((PIECES,)), dma((PIECES,)),
        ],
        compiler_params=pltpu.CompilerParams(
            collective_id=0, has_side_effects=True, vmem_limit_bytes=107 * 2**19
        ),
        name="coupling",
    )(noise, data)
    return (targets, noise_pot[0], data_pot[0])


def solution(mesh):
    placed = (P("row", "col"), P("col", "row"))
    return jax.shard_map(
        per_device,
        mesh=mesh,
        in_specs=placed,
        out_specs=(P(("row", "col"), None), P("row"), P("col")),
        check_vma=False,
    )
```
